32 devices in a mesh: tok: 4 (over z), lat: 8 (over y, x, core).
Axes of the slice: x: 2, y: 2, z: 4, core: 2. Of those that a mesh axis runs over, the one named last changes fastest.
Arguments:
- residuals: bfloat16 [2048, 4096], P('tok', 'lat'), may hold values from -6 to 6
- dictionary: bfloat16 [16384, 4096], P('lat'), may hold values from -0.09375 to 0.09375
- enc_bias: float32 [16384], P('lat'), may hold values from -3 to 3
- dec_bias: float32 [4096], replicated, may hold values from -3 to 3
- tile_ids: int32 [16, 8, 4], P('tok', 'lat'), may hold values from 0 to 31, as said below
- tile_counts: int32 [16, 8], P('tok', 'lat'), may hold values from 0 to 4, as said below
Outputs:
- tile_codes: bfloat16 [16, 8, 4, 8192], P('tok', None, None, 'lat')
- reconstruction: bfloat16 [2048, 4096], P('tok', 'lat')
- decoder_grad: float32 [16384, 4096], P('lat', 'tok')
The draws below stay inside these ranges and needn't reach their ends.
Inputs may be any that keep to these rules, and one draw needn't show every extreme that they name: `tile_ids`: for each token block and latent shard the 4 entries are distinct latent blocks; only the first tile_counts entries count. `tile_counts`: every draw has token blocks with all 4 slots active on every latent shard.
All inputs are finite; a program needn't handle non-finite values.
Results may differ from the reference program's by a relative error of at most 0.02.
Values may be sent and summed in bfloat16 or wider, within the bound.
A program may use at most 128 MiB of HBM per device.

```python
import jax
import jax.numpy as jnp
from jax import lax

D = 4096
LAT_DEV = 2048
TOK_DEV = 512
TILE_ROWS = 128
LAT_TILE = 64
CAP = 4
LATENTS = 16384
TOKENS = 2048
TBLOCKS = 16
LBLOCKS = 32
N_TOK = 4
N_LAT = 8


def draw_tile_ids(key, part):
    key = jax.random.fold_in(key, 11)
    scores = jax.random.randint(key, (TBLOCKS, N_LAT, LBLOCKS), 0, 4096) * LBLOCKS
    scores = scores + jnp.arange(LBLOCKS, dtype=jnp.int32)[None, None, :]
    order = jnp.argsort(scores, axis=-1, stable=True)
    return order[:, :, :CAP].astype(jnp.int32)


def draw_tile_counts(key, part):
    key = jax.random.fold_in(key, 23)
    counts = jax.random.randint(key, (TBLOCKS, N_LAT), 0, CAP + 1)
    block_index = jnp.arange(TBLOCKS, dtype=jnp.int32)[:, None]
    counts = jnp.where(block_index % 5 == 0, CAP, counts)
    return counts.astype(jnp.int32)


def shard_levels(own_key, extent, split, smallest, top_value):
    factor_of, own = 1.0, jax.random.fold_in(own_key, 6)
    for axis_at, parts in split:
        steps = jnp.exp(jax.random.uniform(jax.random.fold_in(own, axis_at), (parts,), jnp.float32, smallest / len(split), top_value / len(split)))
        factor_of = factor_of * jnp.repeat(steps, extent[axis_at] // parts).reshape([-1 if axis == axis_at else 1 for axis in range(len(extent))])
    return factor_of


def centred(stream_key, dims, spread, reach, pieces=(), held_as=jnp.bfloat16):
    gain = shard_levels(stream_key, dims, pieces, -0.22, 0.18) if pieces else 1.0
    entries = jax.random.normal(stream_key, dims, jnp.float32) * spread * gain
    return jnp.minimum(jnp.maximum(entries, -reach), reach).astype(held_as)


def setup_inputs(seed: int = 0) -> dict:
    splits = jax.random.split(jax.random.key(seed), 7)
    residuals = centred(splits[0], (TOKENS, D), 1.0, 6.0, ((0, 4), (1, 8)))
    dictionary = centred(splits[1], (LATENTS, D), D ** -0.5, 0.09375, ((0, 8),))
    enc_bias = centred(splits[2], (LATENTS,), 0.5, 3.0, ((0, 8),), jnp.float32)
    dec_bias = centred(splits[3], (D,), 0.5, 3.0, (), jnp.float32)
    tile_ids = draw_tile_ids(jax.random.fold_in(splits[6], 71), 0)
    tile_counts = draw_tile_counts(jax.random.fold_in(splits[6], 71), 0)
    return {"residuals": residuals, "dictionary": dictionary, "enc_bias": enc_bias, "dec_bias": dec_bias, "tile_ids": tile_ids, "tile_counts": tile_counts}


def reference(residuals, dictionary, enc_bias, dec_bias, tile_ids, tile_counts):
    centered = (residuals.astype(jnp.float32) - dec_bias).astype(jnp.bfloat16)
    live_slots = jnp.arange(CAP, dtype=jnp.int32)[None, None, :] < tile_counts[:, :, None]
    selector = (tile_ids[:, :, :, None] == jnp.arange(LBLOCKS, dtype=jnp.int32)[None, None, None, :]) & live_slots[:, :, :, None]
    tile_active = jnp.any(selector, axis=2).astype(jnp.float32)
    selector_f = selector.astype(jnp.float32)

    def shard_step(running, shard_index):
        weights = lax.dynamic_slice_in_dim(dictionary, shard_index * LAT_DEV, LAT_DEV, 0)
        biases = lax.dynamic_slice_in_dim(enc_bias, shard_index * LAT_DEV, LAT_DEV, 0)
        preact = jnp.dot(centered, weights.T, preferred_element_type=jnp.float32) + biases
        mask_rows = jnp.take(tile_active, shard_index, axis=1)
        code_four = jnp.maximum(preact, 0.0).reshape(TBLOCKS, TILE_ROWS, LBLOCKS, LAT_TILE) * mask_rows[:, None, :, None]
        code_values = code_four.reshape(TOKENS, LAT_DEV).astype(jnp.bfloat16)
        pick_rows = jnp.take(selector_f, shard_index, axis=1)
        picked = jnp.einsum("bcl,brlk->bcrk", pick_rows, code_values.astype(jnp.float32).reshape(TBLOCKS, TILE_ROWS, LBLOCKS, LAT_TILE))
        tile_part = picked.reshape(TBLOCKS, CAP, TILE_ROWS * LAT_TILE).astype(jnp.bfloat16)
        running = running + jnp.dot(code_values, weights, preferred_element_type=jnp.float32)
        return running, (code_values, tile_part)

    start_sum = jnp.zeros((TOKENS, D), jnp.float32)
    total, (all_codes, all_tiles) = lax.scan(shard_step, start_sum, jnp.arange(N_LAT, dtype=jnp.int32))
    recon_full = total + dec_bias
    reconstruction = recon_full.astype(jnp.bfloat16)
    error = (recon_full - residuals.astype(jnp.float32)).astype(jnp.bfloat16)
    error_groups = error.reshape(N_TOK, TOK_DEV, D)

    def grad_step(carry, code_values):
        code_groups = code_values.reshape(N_TOK, TOK_DEV, LAT_DEV)
        summed = jnp.zeros((LAT_DEV, D), jnp.float32)
        for group in range(N_TOK):
            part = jnp.dot(code_groups[group].T, error_groups[group], preferred_element_type=jnp.float32)
            summed = summed + part.astype(jnp.bfloat16).astype(jnp.float32)
        return carry, summed

    unused, grads = lax.scan(grad_step, jnp.zeros((), jnp.float32), all_codes)
    decoder_grad = grads.reshape(LATENTS, D)
    tile_codes = jnp.transpose(all_tiles, (1, 0, 2, 3))
    return tile_codes, reconstruction, decoder_grad
```

```python
import functools

import jax
import jax.numpy as jnp
from jax import lax
from jax.experimental import pallas as pl
from jax.experimental.pallas import tpu as pltpu
from jax.sharding import PartitionSpec as P

TILE_ROWS = 128
LAT_TILE = 64
VMEM_BYTES = 48 * 1024 * 1024


def encode_kernel(cap, ids, counts, res_ref, dec_ref, *rest):
    w_refs, e_refs, out_ref = rest[:cap], rest[cap : 2 * cap], rest[2 * cap]
    b = pl.program_id(0)
    centered = (res_ref[...].astype(jnp.float32) - dec_ref[...]).astype(jnp.bfloat16)
    weights = jnp.concatenate([w[...] for w in w_refs], axis=0)
    preact = lax.dot_general(
        centered, weights, (((1,), (1,)), ((), ())), preferred_element_type=jnp.float32
    )
    bias = jnp.concatenate([e[0] for e in e_refs], axis=1)
    slot = lax.broadcasted_iota(jnp.int32, (1, cap * LAT_TILE), 1) // LAT_TILE
    live = (slot < counts[b]).astype(jnp.float32)
    out_ref[0] = (jnp.maximum(preact + bias, 0.0) * live).astype(jnp.bfloat16)


def encode(gathered, dictionary, enc_bias, dec_bias, ids, counts):
    tok_rows, width = gathered.shape
    blocks, cap = ids.shape
    lat_blocks = dictionary.shape[0] // LAT_TILE
    ids = ids.reshape(-1)
    bias = enc_bias.reshape(lat_blocks, 1, LAT_TILE)

    def row_spec(c):
        return pl.BlockSpec((LAT_TILE, width), lambda b, i, n: (i[b * cap + c], 0))

    def bias_spec(c):
        return pl.BlockSpec((1, 1, LAT_TILE), lambda b, i, n: (i[b * cap + c], 0, 0))

    return pl.pallas_call(
        functools.partial(encode_kernel, cap),
        out_shape=jax.ShapeDtypeStruct((blocks, TILE_ROWS, cap * LAT_TILE), jnp.bfloat16),
        grid_spec=pltpu.PrefetchScalarGridSpec(
            num_scalar_prefetch=2,
            grid=(blocks,),
            in_specs=[
                pl.BlockSpec((TILE_ROWS, width), lambda b, i, n: (b, 0)),
                pl.BlockSpec((1, width), lambda b, i, n: (0, 0)),
            ]
            + [row_spec(c) for c in range(cap)]
            + [bias_spec(c) for c in range(cap)],
            out_specs=pl.BlockSpec((1, TILE_ROWS, cap * LAT_TILE), lambda b, i, n: (b, 0, 0)),
        ),
        compiler_params=pltpu.CompilerParams(vmem_limit_bytes=VMEM_BYTES),
        name="encode",
    )(ids, counts, gathered, dec_bias.reshape(1, -1), *([dictionary] * cap), *([bias] * cap))


def decode_kernel(cap, ids, place, codes_ref, *rest):
    w_refs, out_ref = rest[:cap], rest[cap]
    weights = jnp.concatenate([w[...] for w in w_refs], axis=0)
    part = jnp.dot(codes_ref[0], weights, preferred_element_type=jnp.float32)
    out_ref[...] = part.astype(jnp.bfloat16).reshape(out_ref.shape)


def decode(codes, ids, dictionary, tok_index, width, n_tok, n_lat):
    blocks, _, depth = codes.shape
    cap = depth // LAT_TILE
    per = blocks // n_tok
    rows = per * TILE_ROWS // n_lat
    split = TILE_ROWS // rows

    def row_spec(c):
        return pl.BlockSpec((LAT_TILE, width), lambda b, i, p: (i[b * cap + c], p[0]))

    return pl.pallas_call(
        functools.partial(decode_kernel, cap),
        out_shape=jax.ShapeDtypeStruct((n_lat, n_tok, rows, width), jnp.bfloat16),
        grid_spec=pltpu.PrefetchScalarGridSpec(
            num_scalar_prefetch=2,
            grid=(blocks,),
            in_specs=[pl.BlockSpec((1, TILE_ROWS, depth), lambda b, i, p: (b, 0, 0))]
            + [row_spec(c) for c in range(cap)],
            out_specs=pl.BlockSpec(
                (split, 1, rows, width), lambda b, i, p: (b % per, b // per, 0, 0)
            ),
        ),
        compiler_params=pltpu.CompilerParams(vmem_limit_bytes=VMEM_BYTES),
        name="decode",
    )(ids.reshape(-1), tok_index.reshape(1), codes, *([dictionary] * cap))


def grad_kernel(cap, per, ids, codes_ref, err_ref, out_ref):
    blocks = codes_ref.shape[0]
    split = TILE_ROWS // err_ref.shape[2]
    cols = err_ref.shape[3]
    out_ref[...] = jnp.zeros_like(out_ref)

    @pl.loop(0, blocks)
    def _(b):
        err = err_ref[pl.ds(lax.rem(b, per) * split, split), lax.div(b, per)]
        part = lax.dot_general(
            codes_ref[b],
            err.reshape(TILE_ROWS, cols),
            (((0,), (0,)), ((), ())),
            preferred_element_type=jnp.float32,
        )
        for c in range(cap):
            at = pl.ds(pl.multiple_of(ids[b * cap + c] * LAT_TILE, LAT_TILE), LAT_TILE)
            out_ref[at, :] += part[c * LAT_TILE : (c + 1) * LAT_TILE]


def grad(codes, ids, err, lat_rows):
    blocks, _, depth = codes.shape
    cap = depth // LAT_TILE
    n_lat, n_tok, rows, width = err.shape
    cols = 256
    return pl.pallas_call(
        functools.partial(grad_kernel, cap, blocks // n_tok),
        out_shape=jax.ShapeDtypeStruct((lat_rows, width), jnp.float32),
        grid_spec=pltpu.PrefetchScalarGridSpec(
            num_scalar_prefetch=1,
            grid=(width // cols,),
            in_specs=[
                pl.BlockSpec(codes.shape, lambda j, i: (0, 0, 0)),
                pl.BlockSpec((n_lat, n_tok, rows, cols), lambda j, i: (0, 0, 0, j)),
            ],
            out_specs=pl.BlockSpec((lat_rows, cols), lambda j, i: (0, j)),
        ),
        compiler_params=pltpu.CompilerParams(vmem_limit_bytes=VMEM_BYTES),
        name="grad",
    )(ids.reshape(-1), codes, err)


def body(residuals, dictionary, enc_bias, dec_bias, tile_ids, tile_counts):
    n_tok, n_lat = lax.axis_size("tok"), lax.axis_size("lat")
    tok_index, lat_index = lax.axis_index("tok"), lax.axis_index("lat")
    tok_rows = residuals.shape[0]
    blocks, _, cap = tile_ids.shape
    width = dictionary.shape[1] // n_tok
    rows = tok_rows // n_lat
    ids = tile_ids[:, 0, :]
    ids_all = lax.all_gather(ids, "tok", axis=0, tiled=True)
    gathered = lax.all_gather(residuals, "lat", axis=1, tiled=True)
    codes = encode(gathered, dictionary, enc_bias, dec_bias, ids, tile_counts[:, 0])
    codes_all = lax.all_gather(codes, "tok", axis=0, tiled=True)
    partial_sum = decode(codes_all, ids_all, dictionary, tok_index, width, n_tok, n_lat)
    own_rows = lax.dynamic_slice_in_dim(gathered, lat_index * rows, rows, 0)
    share = lax.all_to_all(
        own_rows.reshape(rows, n_tok, width).transpose(1, 0, 2), "tok", 0, 0, tiled=True
    )
    summed = lax.psum_scatter(partial_sum, "lat", scatter_dimension=0, tiled=False)
    bias = lax.dynamic_slice_in_dim(dec_bias, tok_index * width, width, 0)
    recon = summed.astype(jnp.float32) + bias
    err = (recon - share.astype(jnp.float32)).astype(jnp.bfloat16)
    err_all = lax.all_gather(err, "lat", axis=0, tiled=False)
    decoder_grad = grad(codes_all, ids_all, err_all, dictionary.shape[0])
    back = lax.all_to_all(recon.astype(jnp.bfloat16), "tok", 0, 0, tiled=True)
    back = back.transpose(1, 0, 2).reshape(rows, n_lat, -1).transpose(1, 0, 2)
    reconstruction = lax.all_to_all(back, "lat", 0, 0, tiled=True).reshape(tok_rows, -1)
    sent = codes.reshape(blocks, n_lat, TILE_ROWS // n_lat, cap, LAT_TILE)
    sent = sent.transpose(1, 0, 3, 2, 4).reshape(n_lat, blocks, cap, -1)
    tile_codes = lax.all_to_all(sent, "lat", 0, 0, tiled=True).transpose(1, 0, 2, 3)
    return (tile_codes, reconstruction, decoder_grad)


def solution(mesh):
    placed = (
        P("tok", "lat"),
        P("lat", None),
        P("lat"),
        P(),
        P("tok", "lat", None),
        P("tok", "lat"),
    )
    return jax.shard_map(
        body,
        mesh=mesh,
        in_specs=placed,
        out_specs=(P("tok", None, None, "lat"), P("tok", "lat"), P("lat", "tok")),
        check_vma=False,
    )
```

```python
import functools

import jax
import jax.numpy as jnp
from jax import lax
from jax.experimental import pallas as pl
from jax.experimental.pallas import tpu as pltpu
from jax.sharding import PartitionSpec as P

TILE_ROWS = 128
LAT_TILE = 64
VMEM_BYTES = 48 * 1024 * 1024


def encode_kernel(cap, ids, counts, res_ref, dec_ref, *rest):
    w_refs, e_refs, out_ref = rest[:cap], rest[cap : 2 * cap], rest[2 * cap]
    b = pl.program_id(0)
    centered = (res_ref[...].astype(jnp.float32) - dec_ref[...]).astype(jnp.bfloat16)
    weights = jnp.concatenate([w[...] for w in w_refs], axis=0)
    preact = lax.dot_general(
        centered, weights, (((1,), (1,)), ((), ())), preferred_element_type=jnp.float32
    )
    bias = jnp.concatenate([e[0] for e in e_refs], axis=1)
    slot = lax.broadcasted_iota(jnp.int32, (1, cap * LAT_TILE), 1) // LAT_TILE
    live = (slot < counts[b]).astype(jnp.float32)
    out_ref[0] = (jnp.maximum(preact + bias, 0.0) * live).astype(jnp.bfloat16)


def encode(gathered, dictionary, enc_bias, dec_bias, ids, counts):
    tok_rows, width = gathered.shape
    blocks, cap = ids.shape
    lat_blocks = dictionary.shape[0] // LAT_TILE
    ids = ids.reshape(-1)
    bias = enc_bias.reshape(lat_blocks, 1, LAT_TILE)

    def row_spec(c):
        return pl.BlockSpec((LAT_TILE, width), lambda b, i, n: (i[b * cap + c], 0))

    def bias_spec(c):
        return pl.BlockSpec((1, 1, LAT_TILE), lambda b, i, n: (i[b * cap + c], 0, 0))

    return pl.pallas_call(
        functools.partial(encode_kernel, cap),
        out_shape=jax.ShapeDtypeStruct((blocks, TILE_ROWS, cap * LAT_TILE), jnp.bfloat16),
        grid_spec=pltpu.PrefetchScalarGridSpec(
            num_scalar_prefetch=2,
            grid=(blocks,),
            in_specs=[
                pl.BlockSpec((TILE_ROWS, width), lambda b, i, n: (b, 0)),
                pl.BlockSpec((1, width), lambda b, i, n: (0, 0)),
            ]
            + [row_spec(c) for c in range(cap)]
            + [bias_spec(c) for c in range(cap)],
            out_specs=pl.BlockSpec((1, TILE_ROWS, cap * LAT_TILE), lambda b, i, n: (b, 0, 0)),
        ),
        compiler_params=pltpu.CompilerParams(vmem_limit_bytes=VMEM_BYTES),
        name="encode",
    )(ids, counts, gathered, dec_bias.reshape(1, -1), *([dictionary] * cap), *([bias] * cap))


def decode_kernel(cap, ids, place, codes_ref, *rest):
    w_refs, out_ref = rest[:cap], rest[cap]
    weights = jnp.concatenate([w[...] for w in w_refs], axis=0)
    part = jnp.dot(codes_ref[0], weights, preferred_element_type=jnp.float32)
    out_ref[...] = part.astype(jnp.bfloat16).reshape(out_ref.shape)


def decode(codes, ids, dictionary, tok_index, width, n_tok, n_lat):
    blocks, _, depth = codes.shape
    cap = depth // LAT_TILE
    per = blocks // n_tok
    rows = per * TILE_ROWS // n_lat
    split = TILE_ROWS // rows

    def row_spec(c):
        return pl.BlockSpec((LAT_TILE, width), lambda b, i, p: (i[b * cap + c], p[0]))

    return pl.pallas_call(
        functools.partial(decode_kernel, cap),
        out_shape=jax.ShapeDtypeStruct((n_lat, n_tok, rows, width), jnp.bfloat16),
        grid_spec=pltpu.PrefetchScalarGridSpec(
            num_scalar_prefetch=2,
            grid=(blocks,),
            in_specs=[pl.BlockSpec((1, TILE_ROWS, depth), lambda b, i, p: (b, 0, 0))]
            + [row_spec(c) for c in range(cap)],
            out_specs=pl.BlockSpec(
                (split, 1, rows, width), lambda b, i, p: (b % per, b // per, 0, 0)
            ),
        ),
        compiler_params=pltpu.CompilerParams(vmem_limit_bytes=VMEM_BYTES),
        name="decode",
    )(ids.reshape(-1), tok_index.reshape(1), codes, *([dictionary] * cap))


def grad_kernel(cap, per, ids, codes_ref, err_ref, out_ref):
    blocks = codes_ref.shape[0]
    split = TILE_ROWS // err_ref.shape[2]
    cols = err_ref.shape[3]
    out_ref[...] = jnp.zeros_like(out_ref)

    @pl.loop(0, blocks)
    def _(b):
        err = err_ref[pl.ds(lax.rem(b, per) * split, split), lax.div(b, per)]
        part = lax.dot_general(
            codes_ref[b],
            err.reshape(TILE_ROWS, cols),
            (((0,), (0,)), ((), ())),
            preferred_element_type=jnp.float32,
        )
        for c in range(cap):
            at = pl.ds(pl.multiple_of(ids[b * cap + c] * LAT_TILE, LAT_TILE), LAT_TILE)
            out_ref[at, :] += part[c * LAT_TILE : (c + 1) * LAT_TILE]


def grad(codes, ids, err, lat_rows):
    blocks, _, depth = codes.shape
    cap = depth // LAT_TILE
    n_lat, n_tok, rows, width = err.shape
    cols = 256
    return pl.pallas_call(
        functools.partial(grad_kernel, cap, blocks // n_tok),
        out_shape=jax.ShapeDtypeStruct((lat_rows, width), jnp.float32),
        grid_spec=pltpu.PrefetchScalarGridSpec(
            num_scalar_prefetch=1,
            grid=(width // cols,),
            in_specs=[
                pl.BlockSpec(codes.shape, lambda j, i: (0, 0, 0)),
                pl.BlockSpec((n_lat, n_tok, rows, cols), lambda j, i: (0, 0, 0, j)),
            ],
            out_specs=pl.BlockSpec((lat_rows, cols), lambda j, i: (0, j)),
        ),
        compiler_params=pltpu.CompilerParams(vmem_limit_bytes=VMEM_BYTES),
        name="grad",
    )(ids.reshape(-1), codes, err)


def body(residuals, dictionary, enc_bias, dec_bias, tile_ids, tile_counts):
    n_tok, n_lat = lax.axis_size("tok"), lax.axis_size("lat")
    tok_index, lat_index = lax.axis_index("tok"), lax.axis_index("lat")
    tok_rows = residuals.shape[0]
    blocks, _, cap = tile_ids.shape
    width = dictionary.shape[1] // n_tok
    rows = tok_rows // n_lat
    ids = tile_ids[:, 0, :]
    ids_all = lax.all_gather(tile_ids[:, 0, :], "tok", axis=0, tiled=True).reshape(-1)
    gathered = lax.all_gather(residuals, "lat", axis=1, tiled=True)
    codes = encode(gathered, dictionary, enc_bias, dec_bias, ids, tile_counts[:, 0])
    codes_all = lax.all_gather(codes, "tok", axis=0, tiled=True)
    partial_sum = decode(codes_all, ids_all, dictionary, tok_index, width, n_tok, n_lat)
    own_rows = lax.dynamic_slice_in_dim(gathered, lat_index * rows, rows, 0)
    share = lax.all_to_all(
        own_rows.reshape(rows, n_tok, width).transpose(1, 0, 2), "tok", 0, 0, tiled=True
    )
    summed = lax.psum_scatter(partial_sum, "lat", scatter_dimension=0, tiled=False)
    bias = lax.dynamic_slice_in_dim(dec_bias, tok_index * width, width, 0)
    recon = summed.astype(jnp.float32) + bias
    err = (recon - share.astype(jnp.float32)).astype(jnp.bfloat16)
    err_all = lax.all_gather(err, "lat", axis=0, tiled=False)
    decoder_grad = grad(codes_all, ids_all, err_all, dictionary.shape[0])
    back = lax.all_to_all(recon.astype(jnp.bfloat16), "tok", 0, 0, tiled=True)
    back = back.transpose(1, 0, 2).reshape(rows, n_lat, -1).transpose(1, 0, 2)
    reconstruction = lax.all_to_all(back, "lat", 0, 0, tiled=True).reshape(tok_rows, -1)
    sent = codes.reshape(blocks, n_lat, TILE_ROWS // n_lat, cap, LAT_TILE)
    sent = sent.transpose(1, 0, 3, 2, 4).reshape(n_lat, blocks, cap, -1)
    tile_codes = lax.all_to_all(sent, "lat", 0, 0, tiled=True).transpose(1, 0, 2, 3)
    return (tile_codes, reconstruction, decoder_grad)


def step_kernel(
    cap,
    res_ref, rows_hbm, cols_hbm, enc_ref, dec_ref, live_ref,
    codes_ref, err_ref, tc_ref, rec_ref,
    rows_v, cols_v, gath, mine, sib_out, sib_in, fwd_x, fwd_y, dir_x, dir_y, sum_x, sum_y,
    share, rec, rows_full,
    rows_sem, cols_sem, g_send, g_recv, e_send, e_recv,
    c_send, c_recv, h_send, h_recv, t_send, t_recv, s_send, s_recv, p_send, p_recv,
    b_send, b_recv, r_send, r_recv,
):
    z, lat = lax.axis_index("tok"), lax.axis_index("lat")
    core, chip = lax.rem(lat, 2), lax.div(lat, 2)
    x, y = lax.rem(chip, 2), lax.div(chip, 2)

    def flip(m):
        yy = 1 - y if m & 4 else y
        xx = 1 - x if m & 2 else x
        cc = 1 - core if m & 1 else core
        return (yy * 2 + xx) * 2 + cc

    started = []

    def send(src, dst, send_sem, recv_sem, **where):
        copy = pltpu.make_async_remote_copy(
            src_ref=src, dst_ref=dst, send_sem=send_sem, recv_sem=recv_sem,
            device_id=where, device_id_type=pl.DeviceIdType.MESH,
        )
        copy.start()
        started.append(copy)

    def arrive(dst, send_sem, recv_sem):
        pltpu.make_async_remote_copy(
            src_ref=dst, dst_ref=dst, send_sem=send_sem, recv_sem=recv_sem,
            device_id={"lat": flip(1)}, device_id_type=pl.DeviceIdType.MESH,
        ).wait_recv()

    load_rows = pltpu.make_async_copy(rows_hbm, rows_v, rows_sem)
    load_rows.start()
    load_cols = pltpu.make_async_copy(cols_hbm, cols_v, cols_sem)
    load_cols.start()
    barrier = pltpu.get_barrier_semaphore()
    for m in range(1, 8):
        pl.semaphore_signal(
            barrier, inc=1, device_id={"lat": flip(m)}, device_id_type=pl.DeviceIdType.MESH
        )
    for d in range(1, 4):
        pl.semaphore_signal(
            barrier, inc=1, device_id={"tok": lax.rem(z + d, 4)},
            device_id_type=pl.DeviceIdType.MESH,
        )
    pl.semaphore_wait(barrier, 10)

    def gather_start(ref, own, i, ss, rs):
        send(own, ref.at[lat, i], ss.at[i, 0], rs.at[i, 2], lat=flip(2))
        send(own, ref.at[lat, i], ss.at[i, 1], rs.at[i, 4], lat=flip(4))
        send(own, ref.at[lat, i], ss.at[i, 2], rs.at[i, 1], lat=flip(1))

    def gather_near(ref, i, ss, rs):
        at_x, at_y = ref.at[flip(2), i], ref.at[flip(4), i]
        arrive(at_x, ss.at[i, 0], rs.at[i, 2])
        if i % 2 == 0:
            send(at_x, at_x, ss.at[i, 3], rs.at[i, 6], lat=flip(4))
        send(at_x, at_x, ss.at[i, 4], rs.at[i, 3], lat=flip(1))
        arrive(at_y, ss.at[i, 0], rs.at[i, 4])
        if i % 2 == 1:
            send(at_y, at_y, ss.at[i, 3], rs.at[i, 6], lat=flip(2))
        send(at_y, at_y, ss.at[i, 5], rs.at[i, 5], lat=flip(1))

    def gather_far(ref, i, ss, rs):
        at_d = ref.at[flip(6), i]
        arrive(at_d, ss.at[i, 0], rs.at[i, 6])
        send(at_d, at_d, ss.at[i, 6], rs.at[i, 7], lat=flip(1))

    def gather_end(ref, i, ss, rs):
        for m in (1, 3, 5, 7):
            arrive(ref.at[flip(m), i], ss.at[i, 0], rs.at[i, m])

    for i in range(4):
        gather_start(gath, res_ref.at[i], i, g_send, g_recv)
    for i in range(4):
        gath[lat, i] = res_ref[i]
    gather_near(gath, 0, g_send, g_recv)
    load_rows.wait()

    for i in range(4):
        if i < 3:
            gather_near(gath, i + 1, g_send, g_recv)
        gather_far(gath, i, g_send, g_recv)
        gather_end(gath, i, g_send, g_recv)
        preact = enc_ref[i]
        for s in range(8):
            centered = (gath[s, i].astype(jnp.float32) - dec_ref[s]).astype(jnp.bfloat16)
            weights = rows_v[i, :, s * 512 : (s + 1) * 512]
            preact = preact + lax.dot_general(
                centered, weights, (((1,), (1,)), ((), ())), preferred_element_type=jnp.float32
            )
        codes_ref[z * 4 + i] = (jnp.maximum(preact, 0.0) * live_ref[i]).astype(jnp.bfloat16)
        for d in range(1, 4):
            block = codes_ref.at[z * 4 + i]
            send(block, block, c_send.at[i, d], c_recv.at[i, d], tok=lax.rem(z + d, 4))

    own_rows = pl.ds(pl.multiple_of(core * 64, 64), 64)
    other_rows = pl.ds(pl.multiple_of((1 - core) * 64, 64), 64)
    for d in range(1, 4):
        to = lax.rem(z + d, 4)
        send(
            gath.at[pl.ds(to * 2, 2), chip, own_rows], share.at[z],
            h_send.at[d], h_recv.at[d], tok=to,
        )
    for h in range(2):
        share[z, h] = gath[z * 2 + h, chip, own_rows]

    for i in range(4):
        for d in range(1, 4):
            src = lax.rem(z + 4 - d, 4)
            arrive(codes_ref.at[src * 4 + i], c_send.at[i, d], c_recv.at[i, d])

    load_cols.wait()
    for r, m in enumerate((6, 2, 4, 0)):
        to_chip = lax.div(flip(m), 2)

        @pl.loop(0, 4)
        def _(q):
            block = q * 4 + to_chip
            weights = cols_v[block]
            sib_out[r, q] = jnp.dot(
                codes_ref[block, other_rows, :], weights, preferred_element_type=jnp.float32
            ).astype(jnp.bfloat16)
            mine[r, q] = jnp.dot(
                codes_ref[block, own_rows, :], weights, preferred_element_type=jnp.float32
            ).astype(jnp.bfloat16)

        send(sib_out.at[r], sib_in.at[r], s_send.at[r], s_recv.at[r], lat=flip(1))

    def add(r, q, *more):
        total = mine[r, q].astype(jnp.float32) + sib_in[r, q].astype(jnp.float32)
        for ref in more:
            total = total + ref.astype(jnp.float32)
        return total

    def settle(r, q, *more):
        mine[r, q] = add(r, q, *more).astype(jnp.bfloat16)

    first, second = pl.ds(0, 2), pl.ds(2, 2)
    arrive(sib_in.at[0], s_send.at[0], s_recv.at[0])
    for q in range(4):
        settle(0, q)
    send(mine.at[0, first], fwd_x, p_send.at[0], p_recv.at[0], lat=flip(2))
    send(mine.at[0, second], fwd_y, p_send.at[1], p_recv.at[1], lat=flip(4))
    arrive(sib_in.at[1], s_send.at[1], s_recv.at[1])
    for q in range(2):
        settle(1, q)
    send(mine.at[1, first], dir_x, p_send.at[2], p_recv.at[2], lat=flip(2))
    arrive(sib_in.at[2], s_send.at[2], s_recv.at[2])
    for q in range(2, 4):
        settle(2, q)
    send(mine.at[2, second], dir_y, p_send.at[3], p_recv.at[3], lat=flip(4))
    arrive(fwd_x, p_send.at[0], p_recv.at[0])
    for q in range(2):
        settle(2, q, fwd_x[q])
    send(mine.at[2, first], sum_y, p_send.at[4], p_recv.at[4], lat=flip(4))
    arrive(fwd_y, p_send.at[1], p_recv.at[1])
    for q in range(2, 4):
        settle(1, q, fwd_y[q - 2])
    send(mine.at[1, second], sum_x, p_send.at[5], p_recv.at[5], lat=flip(2))
    arrive(sib_in.at[3], s_send.at[3], s_recv.at[3])
    for d in range(1, 4):
        arrive(share.at[lax.rem(z + 4 - d, 4)], h_send.at[d], h_recv.at[d])

    bias = jnp.concatenate([dec_ref[z * 2], dec_ref[z * 2 + 1]], axis=1)

    def finish(q, *more):
        recon = add(3, q, *more) + bias
        rec[q] = recon.astype(jnp.bfloat16)
        res = jnp.concatenate([share[q, 0], share[q, 1]], axis=1).astype(jnp.float32)
        err_ref[lat, q] = (recon - res).astype(jnp.bfloat16)
        gather_start(err_ref, err_ref.at[lat, q], q, e_send, e_recv)

    arrive(dir_x, p_send.at[2], p_recv.at[2])
    arrive(sum_y, p_send.at[4], p_recv.at[4])
    for q in range(2):
        finish(q, dir_x[q], sum_y[q])
    arrive(dir_y, p_send.at[3], p_recv.at[3])
    arrive(sum_x, p_send.at[5], p_recv.at[5])
    for q in range(2, 4):
        finish(q, dir_y[q - 2], sum_x[q - 2])

    for d in range(1, 4):
        to = lax.rem(z + d, 4)
        send(rec.at[to], rows_full.at[z], b_send.at[d], b_recv.at[d], tok=to)
    rows_full[z] = rec[z]
    gather_near(err_ref, 0, e_send, e_recv)
    gather_near(err_ref, 1, e_send, e_recv)
    for i in range(4):
        if i < 2:
            gather_near(err_ref, i + 2, e_send, e_recv)
        gather_far(err_ref, i, e_send, e_recv)

    own_blocks = pl.ds(z * 4, 4)

    def code_rows(owner):
        return pl.ds(pl.multiple_of(owner * 16, 16), 16)

    for m in range(1, 8):
        to = flip(m)
        send(
            codes_ref.at[own_blocks, code_rows(to), :], tc_ref.at[lat],
            t_send.at[m], t_recv.at[m], lat=to,
        )
    tc_ref[lat] = codes_ref[own_blocks, code_rows(lat), :]
    for d in range(1, 4):
        src = lax.rem(z + 4 - d, 4)
        arrive(rows_full.at[src], b_send.at[d], b_recv.at[d])

    def columns(owner):
        return pl.ds(pl.multiple_of(lax.rem(owner, 2) * 512, 512), 512)

    for m in range(1, 8):
        to = flip(m)
        send(
            rows_full.at[lax.div(to, 2), :, columns(to)], rec_ref.at[lat],
            r_send.at[m], r_recv.at[m], lat=to,
        )
    rec_ref[lat] = rows_full[chip, :, columns(lat)]
    for i in range(4):
        gather_end(err_ref, i, e_send, e_recv)
    for m in range(1, 8):
        arrive(tc_ref.at[flip(m)], t_send.at[m], t_recv.at[m])
        arrive(rec_ref.at[flip(m)], r_send.at[m], r_recv.at[m])
    for copy in started:
        copy.wait_send()


def select_kernel(cap, ids, ids_all, dict_hbm, rows_hbm, cols_hbm, rows_sem, cols_sem):
    z = lax.axis_index("tok")
    width = cols_hbm.shape[2]
    columns = pl.ds(pl.multiple_of(z * width, width), width)
    copies = []
    for ref, out, sem, part in (
        (ids, rows_hbm, rows_sem, None), (ids_all, cols_hbm, cols_sem, columns)
    ):
        for n in range(out.shape[0] * cap):
            at = pl.ds(pl.multiple_of(ref[n] * LAT_TILE, LAT_TILE), LAT_TILE)
            to = pl.ds((n % cap) * LAT_TILE, LAT_TILE)
            src = dict_hbm.at[at] if part is None else dict_hbm.at[at, part]
            copy = pltpu.make_async_copy(src, out.at[n // cap, to], sem.at[n])
            copy.start()
            copies.append(copy)
    for copy in copies:
        copy.wait()


def select(ids, ids_all, dictionary, cap, width):
    depth = cap * LAT_TILE
    anywhere = pl.BlockSpec(memory_space=pl.ANY)
    smem = pl.BlockSpec(memory_space=pltpu.SMEM)
    return pl.pallas_call(
        functools.partial(select_kernel, cap),
        out_shape=[
            jax.ShapeDtypeStruct((ids.size // cap, depth, dictionary.shape[1]), jnp.bfloat16),
            jax.ShapeDtypeStruct((ids_all.size // cap, depth, width), jnp.bfloat16),
        ],
        in_specs=[smem, smem, anywhere],
        out_specs=[anywhere, anywhere],
        scratch_shapes=[
            pltpu.SemaphoreType.DMA((ids.size,)),
            pltpu.SemaphoreType.DMA((ids_all.size,)),
        ],
        name="select",
    )(ids, ids_all, dictionary)


def small_body(residuals, dictionary, enc_bias, dec_bias, tile_ids, tile_counts):
    cap = tile_ids.shape[2]
    lat_rows, model = dictionary.shape
    ids = tile_ids.reshape(-1)
    ids_all = lax.all_gather(tile_ids[:, 0, :], "tok", axis=0, tiled=True).reshape(-1)
    rows_sel, cols_sel = select(ids, ids_all, dictionary, cap, 1024)
    bias = enc_bias.reshape(-1, LAT_TILE)[ids].reshape(4, 1, cap * LAT_TILE)
    live = jnp.arange(cap, dtype=jnp.int32)[None, :] < tile_counts
    live = jnp.repeat(live.astype(jnp.float32), LAT_TILE, axis=1).reshape(4, 1, cap * LAT_TILE)
    bf16, f32, dma = jnp.bfloat16, jnp.float32, pltpu.SemaphoreType.DMA
    vmem, anywhere = pl.BlockSpec(memory_space=pltpu.VMEM), pl.BlockSpec(memory_space=pl.ANY)
    codes_all, err_all, tiles, recon = pl.pallas_call(
        functools.partial(step_kernel, cap),
        out_shape=[
            jax.ShapeDtypeStruct((16, 128, cap * LAT_TILE), bf16),
            jax.ShapeDtypeStruct((8, 4, 64, 1024), bf16),
            jax.ShapeDtypeStruct((8, 4, 16, cap * LAT_TILE), bf16),
            jax.ShapeDtypeStruct((8, 64, 512), bf16),
        ],
        in_specs=[vmem, anywhere, anywhere, vmem, vmem, vmem],
        out_specs=[vmem, vmem, vmem, vmem],
        scratch_shapes=[
            pltpu.VMEM(rows_sel.shape, bf16),
            pltpu.VMEM(cols_sel.shape, bf16),
            pltpu.VMEM((8, 4, 128, 512), bf16),
            pltpu.VMEM((4, 4, 64, 1024), bf16),
            pltpu.VMEM((4, 4, 64, 1024), bf16),
            pltpu.VMEM((4, 4, 64, 1024), bf16),
        ]
        + [pltpu.VMEM((2, 64, 1024), bf16)] * 6
        + [
            pltpu.VMEM((4, 2, 64, 512), bf16),
            pltpu.VMEM((4, 64, 1024), bf16),
            pltpu.VMEM((4, 64, 1024), bf16),
            dma, dma,
            dma((4, 7)), dma((4, 8)), dma((4, 7)), dma((4, 8)),
            dma((4, 4)), dma((4, 4)),
            dma((4,)), dma((4,)),
            dma((8,)), dma((8,)),
            dma((4,)), dma((4,)),
            dma((6,)), dma((6,)),
            dma((4,)), dma((4,)),
            dma((8,)), dma((8,)),
        ],
        compiler_params=pltpu.CompilerParams(
            collective_id=0, has_side_effects=True, vmem_limit_bytes=VMEM_BYTES
        ),
        name="step",
    )(
        residuals.reshape(4, 128, 512),
        rows_sel,
        cols_sel,
        bias,
        dec_bias.reshape(8, 1, 512),
        live,
    )
    decoder_grad = grad(codes_all, ids_all, err_all, lat_rows)
    tiles = tiles.reshape(8, 4, 16, cap, LAT_TILE).transpose(1, 0, 3, 2, 4).reshape(4, 8, cap, -1)
    return tiles, recon.reshape(512, 512), decoder_grad


def solution(mesh):
    sizes = dict(mesh.shape)
    chosen = small_body if sizes == {"tok": 4, "lat": 8} else body
    placed = (
        P("tok", "lat"),
        P("lat", None),
        P("lat"),
        P(),
        P("tok", "lat", None),
        P("tok", "lat"),
    )
    return jax.shard_map(
        chosen,
        mesh=mesh,
        in_specs=placed,
        out_specs=(P("tok", None, None, "lat"), P("tok", "lat"), P("lat", "tok")),
        check_vma=False,
    )
```

```python
import functools

import jax
import jax.numpy as jnp
from jax import lax
from jax.experimental import pallas as pl
from jax.experimental.pallas import tpu as pltpu
from jax.sharding import PartitionSpec as P

TILE_ROWS = 128
LAT_TILE = 64
VMEM_BYTES = 48 * 1024 * 1024


def encode_kernel(cap, ids, counts, res_ref, dec_ref, *rest):
    w_refs, e_refs, out_ref = rest[:cap], rest[cap : 2 * cap], rest[2 * cap]
    b = pl.program_id(0)
    centered = (res_ref[...].astype(jnp.float32) - dec_ref[...]).astype(jnp.bfloat16)
    weights = jnp.concatenate([w[...] for w in w_refs], axis=0)
    preact = lax.dot_general(
        centered, weights, (((1,), (1,)), ((), ())), preferred_element_type=jnp.float32
    )
    bias = jnp.concatenate([e[0] for e in e_refs], axis=1)
    slot = lax.broadcasted_iota(jnp.int32, (1, cap * LAT_TILE), 1) // LAT_TILE
    live = (slot < counts[b]).astype(jnp.float32)
    out_ref[0] = (jnp.maximum(preact + bias, 0.0) * live).astype(jnp.bfloat16)


def encode(gathered, dictionary, enc_bias, dec_bias, ids, counts):
    tok_rows, width = gathered.shape
    blocks, cap = ids.shape
    lat_blocks = dictionary.shape[0] // LAT_TILE
    ids = ids.reshape(-1)
    bias = enc_bias.reshape(lat_blocks, 1, LAT_TILE)

    def row_spec(c):
        return pl.BlockSpec((LAT_TILE, width), lambda b, i, n: (i[b * cap + c], 0))

    def bias_spec(c):
        return pl.BlockSpec((1, 1, LAT_TILE), lambda b, i, n: (i[b * cap + c], 0, 0))

    return pl.pallas_call(
        functools.partial(encode_kernel, cap),
        out_shape=jax.ShapeDtypeStruct((blocks, TILE_ROWS, cap * LAT_TILE), jnp.bfloat16),
        grid_spec=pltpu.PrefetchScalarGridSpec(
            num_scalar_prefetch=2,
            grid=(blocks,),
            in_specs=[
                pl.BlockSpec((TILE_ROWS, width), lambda b, i, n: (b, 0)),
                pl.BlockSpec((1, width), lambda b, i, n: (0, 0)),
            ]
            + [row_spec(c) for c in range(cap)]
            + [bias_spec(c) for c in range(cap)],
            out_specs=pl.BlockSpec((1, TILE_ROWS, cap * LAT_TILE), lambda b, i, n: (b, 0, 0)),
        ),
        compiler_params=pltpu.CompilerParams(vmem_limit_bytes=VMEM_BYTES),
        name="encode",
    )(ids, counts, gathered, dec_bias.reshape(1, -1), *([dictionary] * cap), *([bias] * cap))


def decode_kernel(cap, ids, place, codes_ref, *rest):
    w_refs, out_ref = rest[:cap], rest[cap]
    weights = jnp.concatenate([w[...] for w in w_refs], axis=0)
    part = jnp.dot(codes_ref[0], weights, preferred_element_type=jnp.float32)
    out_ref[...] = part.astype(jnp.bfloat16).reshape(out_ref.shape)


def decode(codes, ids, dictionary, tok_index, width, n_tok, n_lat):
    blocks, _, depth = codes.shape
    cap = depth // LAT_TILE
    per = blocks // n_tok
    rows = per * TILE_ROWS // n_lat
    split = TILE_ROWS // rows

    def row_spec(c):
        return pl.BlockSpec((LAT_TILE, width), lambda b, i, p: (i[b * cap + c], p[0]))

    return pl.pallas_call(
        functools.partial(decode_kernel, cap),
        out_shape=jax.ShapeDtypeStruct((n_lat, n_tok, rows, width), jnp.bfloat16),
        grid_spec=pltpu.PrefetchScalarGridSpec(
            num_scalar_prefetch=2,
            grid=(blocks,),
            in_specs=[pl.BlockSpec((1, TILE_ROWS, depth), lambda b, i, p: (b, 0, 0))]
            + [row_spec(c) for c in range(cap)],
            out_specs=pl.BlockSpec(
                (split, 1, rows, width), lambda b, i, p: (b % per, b // per, 0, 0)
            ),
        ),
        compiler_params=pltpu.CompilerParams(vmem_limit_bytes=VMEM_BYTES),
        name="decode",
    )(ids.reshape(-1), tok_index.reshape(1), codes, *([dictionary] * cap))


def grad_kernel(cap, per, ids, codes_ref, err_ref, out_ref):
    blocks = codes_ref.shape[0]
    split = TILE_ROWS // err_ref.shape[2]
    cols = err_ref.shape[3]
    out_ref[...] = jnp.zeros_like(out_ref)

    @pl.loop(0, blocks)
    def _(b):
        err = err_ref[pl.ds(lax.rem(b, per) * split, split), lax.div(b, per)]
        part = lax.dot_general(
            codes_ref[b],
            err.reshape(TILE_ROWS, cols),
            (((0,), (0,)), ((), ())),
            preferred_element_type=jnp.float32,
        )
        for c in range(cap):
            at = pl.ds(pl.multiple_of(ids[b * cap + c] * LAT_TILE, LAT_TILE), LAT_TILE)
            out_ref[at, :] += part[c * LAT_TILE : (c + 1) * LAT_TILE]


def grad(codes, ids, err, lat_rows):
    blocks, _, depth = codes.shape
    cap = depth // LAT_TILE
    n_lat, n_tok, rows, width = err.shape
    cols = 256
    return pl.pallas_call(
        functools.partial(grad_kernel, cap, blocks // n_tok),
        out_shape=jax.ShapeDtypeStruct((lat_rows, width), jnp.float32),
        grid_spec=pltpu.PrefetchScalarGridSpec(
            num_scalar_prefetch=1,
            grid=(width // cols,),
            in_specs=[
                pl.BlockSpec(codes.shape, lambda j, i: (0, 0, 0)),
                pl.BlockSpec((n_lat, n_tok, rows, cols), lambda j, i: (0, 0, 0, j)),
            ],
            out_specs=pl.BlockSpec((lat_rows, cols), lambda j, i: (0, j)),
        ),
        compiler_params=pltpu.CompilerParams(vmem_limit_bytes=VMEM_BYTES),
        name="grad",
    )(ids.reshape(-1), codes, err)


def body(residuals, dictionary, enc_bias, dec_bias, tile_ids, tile_counts):
    n_tok, n_lat = lax.axis_size("tok"), lax.axis_size("lat")
    tok_index, lat_index = lax.axis_index("tok"), lax.axis_index("lat")
    tok_rows = residuals.shape[0]
    blocks, _, cap = tile_ids.shape
    width = dictionary.shape[1] // n_tok
    rows = tok_rows // n_lat
    ids = tile_ids[:, 0, :]
    ids_all = lax.all_gather(tile_ids[:, 0, :], "tok", axis=0, tiled=True).reshape(-1)
    gathered = lax.all_gather(residuals, "lat", axis=1, tiled=True)
    codes = encode(gathered, dictionary, enc_bias, dec_bias, ids, tile_counts[:, 0])
    codes_all = lax.all_gather(codes, "tok", axis=0, tiled=True)
    partial_sum = decode(codes_all, ids_all, dictionary, tok_index, width, n_tok, n_lat)
    own_rows = lax.dynamic_slice_in_dim(gathered, lat_index * rows, rows, 0)
    share = lax.all_to_all(
        own_rows.reshape(rows, n_tok, width).transpose(1, 0, 2), "tok", 0, 0, tiled=True
    )
    summed = lax.psum_scatter(partial_sum, "lat", scatter_dimension=0, tiled=False)
    bias = lax.dynamic_slice_in_dim(dec_bias, tok_index * width, width, 0)
    recon = summed.astype(jnp.float32) + bias
    err = (recon - share.astype(jnp.float32)).astype(jnp.bfloat16)
    err_all = lax.all_gather(err, "lat", axis=0, tiled=False)
    decoder_grad = grad(codes_all, ids_all, err_all, dictionary.shape[0])
    back = lax.all_to_all(recon.astype(jnp.bfloat16), "tok", 0, 0, tiled=True)
    back = back.transpose(1, 0, 2).reshape(rows, n_lat, -1).transpose(1, 0, 2)
    reconstruction = lax.all_to_all(back, "lat", 0, 0, tiled=True).reshape(tok_rows, -1)
    sent = codes.reshape(blocks, n_lat, TILE_ROWS // n_lat, cap, LAT_TILE)
    sent = sent.transpose(1, 0, 3, 2, 4).reshape(n_lat, blocks, cap, -1)
    tile_codes = lax.all_to_all(sent, "lat", 0, 0, tiled=True).transpose(1, 0, 2, 3)
    return (tile_codes, reconstruction, decoder_grad)


def step_kernel(
    cap,
    res_ref, rows_hbm, cols_hbm, enc_ref, dec_ref, live_ref,
    codes_ref, err_ref, tc_ref, rec_ref,
    rows_v, cols_v, gath, mine, sib_out, sib_in, fwd_x, fwd_y, dir_x, dir_y, sum_x, sum_y,
    share, rec, rows_full,
    rows_sem, cols_sem, g_send, g_recv, e_send, e_recv,
    c_send, c_recv, h_send, h_recv, t_send, t_recv, s_send, s_recv, p_send, p_recv,
    b_send, b_recv, r_send, r_recv,
):
    z, lat = lax.axis_index("tok"), lax.axis_index("lat")
    core, chip = lax.rem(lat, 2), lax.div(lat, 2)
    x, y = lax.rem(chip, 2), lax.div(chip, 2)

    def flip(m):
        yy = 1 - y if m & 4 else y
        xx = 1 - x if m & 2 else x
        cc = 1 - core if m & 1 else core
        return (yy * 2 + xx) * 2 + cc

    started = []

    def send(src, dst, send_sem, recv_sem, **where):
        copy = pltpu.make_async_remote_copy(
            src_ref=src, dst_ref=dst, send_sem=send_sem, recv_sem=recv_sem,
            device_id=where, device_id_type=pl.DeviceIdType.MESH,
        )
        copy.start()
        started.append(copy)

    def arrive(dst, send_sem, recv_sem):
        pltpu.make_async_remote_copy(
            src_ref=dst, dst_ref=dst, send_sem=send_sem, recv_sem=recv_sem,
            device_id={"lat": flip(1)}, device_id_type=pl.DeviceIdType.MESH,
        ).wait_recv()

    load_rows = pltpu.make_async_copy(rows_hbm, rows_v, rows_sem)
    load_rows.start()
    load_cols = pltpu.make_async_copy(cols_hbm, cols_v, cols_sem)
    load_cols.start()
    barrier = pltpu.get_barrier_semaphore()
    for m in range(1, 8):
        pl.semaphore_signal(
            barrier, inc=1, device_id={"lat": flip(m)}, device_id_type=pl.DeviceIdType.MESH
        )
    for d in range(1, 4):
        pl.semaphore_signal(
            barrier, inc=1, device_id={"tok": lax.rem(z + d, 4)},
            device_id_type=pl.DeviceIdType.MESH,
        )
    pl.semaphore_wait(barrier, 10)

    def gather_start(ref, own, i, ss, rs):
        send(own, ref.at[lat, i], ss.at[i, 0], rs.at[i, 2], lat=flip(2))
        send(own, ref.at[lat, i], ss.at[i, 1], rs.at[i, 4], lat=flip(4))
        send(own, ref.at[lat, i], ss.at[i, 2], rs.at[i, 1], lat=flip(1))

    def gather_near(ref, i, ss, rs):
        at_x, at_y = ref.at[flip(2), i], ref.at[flip(4), i]
        arrive(at_x, ss.at[i, 0], rs.at[i, 2])
        if i % 2 == 0:
            send(at_x, at_x, ss.at[i, 3], rs.at[i, 6], lat=flip(4))
        send(at_x, at_x, ss.at[i, 4], rs.at[i, 3], lat=flip(1))
        arrive(at_y, ss.at[i, 0], rs.at[i, 4])
        if i % 2 == 1:
            send(at_y, at_y, ss.at[i, 3], rs.at[i, 6], lat=flip(2))
        send(at_y, at_y, ss.at[i, 5], rs.at[i, 5], lat=flip(1))

    def gather_far(ref, i, ss, rs):
        at_d = ref.at[flip(6), i]
        arrive(at_d, ss.at[i, 0], rs.at[i, 6])
        send(at_d, at_d, ss.at[i, 6], rs.at[i, 7], lat=flip(1))

    def gather_end(ref, i, ss, rs):
        for m in (1, 3, 5, 7):
            arrive(ref.at[flip(m), i], ss.at[i, 0], rs.at[i, m])

    for i in range(4):
        gather_start(gath, res_ref.at[i], i, g_send, g_recv)
    for i in range(4):
        gath[lat, i] = res_ref[i]
    gather_near(gath, 0, g_send, g_recv)
    load_rows.wait()

    for i in range(4):
        if i < 3:
            gather_near(gath, i + 1, g_send, g_recv)
        gather_far(gath, i, g_send, g_recv)
        gather_end(gath, i, g_send, g_recv)
        preact = enc_ref[i]
        for s in range(8):
            centered = (gath[s, i].astype(jnp.float32) - dec_ref[s]).astype(jnp.bfloat16)
            weights = rows_v[i, :, s * 512 : (s + 1) * 512]
            preact = preact + lax.dot_general(
                centered, weights, (((1,), (1,)), ((), ())), preferred_element_type=jnp.float32
            )
        codes_ref[z * 4 + i] = (jnp.maximum(preact, 0.0) * live_ref[i]).astype(jnp.bfloat16)
        for d in range(1, 4):
            block = codes_ref.at[z * 4 + i]
            send(block, block, c_send.at[i, d], c_recv.at[i, d], tok=lax.rem(z + d, 4))

    own_rows = pl.ds(pl.multiple_of(core * 64, 64), 64)
    other_rows = pl.ds(pl.multiple_of((1 - core) * 64, 64), 64)
    for d in range(1, 4):
        to = lax.rem(z + d, 4)
        send(
            gath.at[pl.ds(to * 2, 2), chip, own_rows], share.at[z],
            h_send.at[d], h_recv.at[d], tok=to,
        )
    for h in range(2):
        share[z, h] = gath[z * 2 + h, chip, own_rows]

    for i in range(4):
        for d in range(1, 4):
            src = lax.rem(z + 4 - d, 4)
            arrive(codes_ref.at[src * 4 + i], c_send.at[i, d], c_recv.at[i, d])

    load_cols.wait()
    for r, m in enumerate((6, 2, 4, 0)):
        to_chip = lax.div(flip(m), 2)

        @pl.loop(0, 4)
        def _(q):
            block = q * 4 + to_chip
            weights = cols_v[block]
            sib_out[r, q] = jnp.dot(
                codes_ref[block, other_rows, :], weights, preferred_element_type=jnp.float32
            ).astype(jnp.bfloat16)
            mine[r, q] = jnp.dot(
                codes_ref[block, own_rows, :], weights, preferred_element_type=jnp.float32
            ).astype(jnp.bfloat16)

        send(sib_out.at[r], sib_in.at[r], s_send.at[r], s_recv.at[r], lat=flip(1))

    def add(r, q, *more):
        total = mine[r, q].astype(jnp.float32) + sib_in[r, q].astype(jnp.float32)
        for ref in more:
            total = total + ref.astype(jnp.float32)
        return total

    def settle(r, q, *more):
        mine[r, q] = add(r, q, *more).astype(jnp.bfloat16)

    first, second = pl.ds(0, 2), pl.ds(2, 2)
    arrive(sib_in.at[0], s_send.at[0], s_recv.at[0])
    for q in range(4):
        settle(0, q)
    send(mine.at[0, first], fwd_x, p_send.at[0], p_recv.at[0], lat=flip(2))
    send(mine.at[0, second], fwd_y, p_send.at[1], p_recv.at[1], lat=flip(4))
    arrive(sib_in.at[1], s_send.at[1], s_recv.at[1])
    for q in range(2):
        settle(1, q)
    send(mine.at[1, first], dir_x, p_send.at[2], p_recv.at[2], lat=flip(2))
    arrive(sib_in.at[2], s_send.at[2], s_recv.at[2])
    for q in range(2, 4):
        settle(2, q)
    send(mine.at[2, second], dir_y, p_send.at[3], p_recv.at[3], lat=flip(4))
    arrive(fwd_x, p_send.at[0], p_recv.at[0])
    for q in range(2):
        settle(2, q, fwd_x[q])
    send(mine.at[2, first], sum_y, p_send.at[4], p_recv.at[4], lat=flip(4))
    arrive(fwd_y, p_send.at[1], p_recv.at[1])
    for q in range(2, 4):
        settle(1, q, fwd_y[q - 2])
    send(mine.at[1, second], sum_x, p_send.at[5], p_recv.at[5], lat=flip(2))
    arrive(sib_in.at[3], s_send.at[3], s_recv.at[3])
    for d in range(1, 4):
        arrive(share.at[lax.rem(z + 4 - d, 4)], h_send.at[d], h_recv.at[d])

    bias = jnp.concatenate([dec_ref[z * 2], dec_ref[z * 2 + 1]], axis=1)

    def finish(q, *more):
        recon = add(3, q, *more) + bias
        rec[q] = recon.astype(jnp.bfloat16)
        res = jnp.concatenate([share[q, 0], share[q, 1]], axis=1).astype(jnp.float32)
        err_ref[lat, q] = (recon - res).astype(jnp.bfloat16)
        gather_start(err_ref, err_ref.at[lat, q], q, e_send, e_recv)

    arrive(dir_x, p_send.at[2], p_recv.at[2])
    arrive(sum_y, p_send.at[4], p_recv.at[4])
    for q in range(2):
        finish(q, dir_x[q], sum_y[q])
    arrive(dir_y, p_send.at[3], p_recv.at[3])
    arrive(sum_x, p_send.at[5], p_recv.at[5])
    for q in range(2, 4):
        finish(q, dir_y[q - 2], sum_x[q - 2])

    for d in range(1, 4):
        to = lax.rem(z + d, 4)
        send(rec.at[to], rows_full.at[z], b_send.at[d], b_recv.at[d], tok=to)
    rows_full[z] = rec[z]
    gather_near(err_ref, 0, e_send, e_recv)
    gather_near(err_ref, 1, e_send, e_recv)
    for i in range(4):
        if i < 2:
            gather_near(err_ref, i + 2, e_send, e_recv)
        gather_far(err_ref, i, e_send, e_recv)

    own_blocks = pl.ds(z * 4, 4)

    def code_rows(owner):
        return pl.ds(pl.multiple_of(owner * 16, 16), 16)

    for m in range(1, 8):
        to = flip(m)
        send(
            codes_ref.at[own_blocks, code_rows(to), :], tc_ref.at[lat],
            t_send.at[m], t_recv.at[m], lat=to,
        )
    tc_ref[lat] = codes_ref[own_blocks, code_rows(lat), :]
    for d in range(1, 4):
        src = lax.rem(z + 4 - d, 4)
        arrive(rows_full.at[src], b_send.at[d], b_recv.at[d])

    def columns(owner):
        return pl.ds(pl.multiple_of(lax.rem(owner, 2) * 512, 512), 512)

    for m in range(1, 8):
        to = flip(m)
        send(
            rows_full.at[lax.div(to, 2), :, columns(to)], rec_ref.at[lat],
            r_send.at[m], r_recv.at[m], lat=to,
        )
    rec_ref[lat] = rows_full[chip, :, columns(lat)]
    for i in range(4):
        gather_end(err_ref, i, e_send, e_recv)
    for m in range(1, 8):
        arrive(tc_ref.at[flip(m)], t_send.at[m], t_recv.at[m])
        arrive(rec_ref.at[flip(m)], r_send.at[m], r_recv.at[m])
    for copy in started:
        copy.wait_send()


def select_kernel(ids, place, *refs):
    out_ref = refs[-1]
    for n, ref in enumerate(refs[:-1]):
        at = (n * LAT_TILE) % out_ref.shape[1]
        out_ref[n * LAT_TILE // out_ref.shape[1], at : at + LAT_TILE] = ref[...]


def select(ids, place, dictionary, cap, group, width):
    blocks, depth = ids.size // cap, cap * LAT_TILE

    def row_spec(n):
        return pl.BlockSpec((LAT_TILE, width), lambda b, i, p: (i[b * group * cap + n], p[0]))

    return pl.pallas_call(
        select_kernel,
        out_shape=jax.ShapeDtypeStruct((blocks, depth, width), jnp.bfloat16),
        grid_spec=pltpu.PrefetchScalarGridSpec(
            num_scalar_prefetch=2,
            grid=(blocks // group,),
            in_specs=[row_spec(n) for n in range(group * cap)],
            out_specs=pl.BlockSpec((group, depth, width), lambda b, i, p: (b, 0, 0)),
        ),
        compiler_params=pltpu.CompilerParams(vmem_limit_bytes=VMEM_BYTES),
        name="select",
    )(ids, place.reshape(1), *([dictionary] * (group * cap)))


def small_body(residuals, dictionary, enc_bias, dec_bias, tile_ids, tile_counts):
    cap = tile_ids.shape[2]
    lat_rows, model = dictionary.shape
    ids = tile_ids.reshape(-1)
    ids_all = lax.all_gather(tile_ids[:, 0, :], "tok", axis=0, tiled=True).reshape(-1)
    rows_sel = select(ids, jnp.zeros((), jnp.int32), dictionary, cap, 1, model)
    cols_sel = select(ids_all, lax.axis_index("tok"), dictionary, cap, 2, 1024)
    bias = enc_bias.reshape(-1, LAT_TILE)[ids].reshape(4, 1, cap * LAT_TILE)
    live = jnp.arange(cap, dtype=jnp.int32)[None, :] < tile_counts
    live = jnp.repeat(live.astype(jnp.float32), LAT_TILE, axis=1).reshape(4, 1, cap * LAT_TILE)
    bf16, f32, dma = jnp.bfloat16, jnp.float32, pltpu.SemaphoreType.DMA
    vmem, anywhere = pl.BlockSpec(memory_space=pltpu.VMEM), pl.BlockSpec(memory_space=pl.ANY)
    codes_all, err_all, tiles, recon = pl.pallas_call(
        functools.partial(step_kernel, cap),
        out_shape=[
            jax.ShapeDtypeStruct((16, 128, cap * LAT_TILE), bf16),
            jax.ShapeDtypeStruct((8, 4, 64, 1024), bf16),
            jax.ShapeDtypeStruct((8, 4, 16, cap * LAT_TILE), bf16),
            jax.ShapeDtypeStruct((8, 64, 512), bf16),
        ],
        in_specs=[vmem, anywhere, anywhere, vmem, vmem, vmem],
        out_specs=[vmem, vmem, vmem, vmem],
        scratch_shapes=[
            pltpu.VMEM(rows_sel.shape, bf16),
            pltpu.VMEM(cols_sel.shape, bf16),
            pltpu.VMEM((8, 4, 128, 512), bf16),
            pltpu.VMEM((4, 4, 64, 1024), bf16),
            pltpu.VMEM((4, 4, 64, 1024), bf16),
            pltpu.VMEM((4, 4, 64, 1024), bf16),
        ]
        + [pltpu.VMEM((2, 64, 1024), bf16)] * 6
        + [
            pltpu.VMEM((4, 2, 64, 512), bf16),
            pltpu.VMEM((4, 64, 1024), bf16),
            pltpu.VMEM((4, 64, 1024), bf16),
            dma, dma,
            dma((4, 7)), dma((4, 8)), dma((4, 7)), dma((4, 8)),
            dma((4, 4)), dma((4, 4)),
            dma((4,)), dma((4,)),
            dma((8,)), dma((8,)),
            dma((4,)), dma((4,)),
            dma((6,)), dma((6,)),
            dma((4,)), dma((4,)),
            dma((8,)), dma((8,)),
        ],
        compiler_params=pltpu.CompilerParams(
            collective_id=0, has_side_effects=True, vmem_limit_bytes=VMEM_BYTES
        ),
        name="step",
    )(
        residuals.reshape(4, 128, 512),
        rows_sel,
        cols_sel,
        bias,
        dec_bias.reshape(8, 1, 512),
        live,
    )
    decoder_grad = grad(codes_all, ids_all, err_all, lat_rows)
    tiles = tiles.reshape(8, 4, 16, cap, LAT_TILE).transpose(1, 0, 3, 2, 4).reshape(4, 8, cap, -1)
    return tiles, recon.reshape(512, 512), decoder_grad


def solution(mesh):
    sizes = dict(mesh.shape)
    chosen = small_body if sizes == {"tok": 4, "lat": 8} else body
    placed = (
        P("tok", "lat"),
        P("lat", None),
        P("lat"),
        P(),
        P("tok", "lat", None),
        P("tok", "lat"),
    )
    return jax.shard_map(
        chosen,
        mesh=mesh,
        in_specs=placed,
        out_specs=(P("tok", None, None, "lat"), P("tok", "lat"), P("lat", "tok")),
        check_vma=False,
    )
```

```python
import functools

import jax
import jax.numpy as jnp
from jax import lax
from jax.experimental import pallas as pl
from jax.experimental.pallas import tpu as pltpu
from jax.sharding import PartitionSpec as P

TILE_ROWS = 128
LAT_TILE = 64
VMEM_BYTES = 48 * 1024 * 1024


def encode_kernel(cap, ids, counts, res_ref, dec_ref, *rest):
    w_refs, e_refs, out_ref = rest[:cap], rest[cap : 2 * cap], rest[2 * cap]
    b = pl.program_id(0)
    centered = (res_ref[...].astype(jnp.float32) - dec_ref[...]).astype(jnp.bfloat16)
    weights = jnp.concatenate([w[...] for w in w_refs], axis=0)
    preact = lax.dot_general(
        centered, weights, (((1,), (1,)), ((), ())), preferred_element_type=jnp.float32
    )
    bias = jnp.concatenate([e[0] for e in e_refs], axis=1)
    slot = lax.broadcasted_iota(jnp.int32, (1, cap * LAT_TILE), 1) // LAT_TILE
    live = (slot < counts[b]).astype(jnp.float32)
    out_ref[0] = (jnp.maximum(preact + bias, 0.0) * live).astype(jnp.bfloat16)


def encode(gathered, dictionary, enc_bias, dec_bias, ids, counts):
    tok_rows, width = gathered.shape
    blocks, cap = ids.shape
    lat_blocks = dictionary.shape[0] // LAT_TILE
    ids = ids.reshape(-1)
    bias = enc_bias.reshape(lat_blocks, 1, LAT_TILE)

    def row_spec(c):
        return pl.BlockSpec((LAT_TILE, width), lambda b, i, n: (i[b * cap + c], 0))

    def bias_spec(c):
        return pl.BlockSpec((1, 1, LAT_TILE), lambda b, i, n: (i[b * cap + c], 0, 0))

    return pl.pallas_call(
        functools.partial(encode_kernel, cap),
        out_shape=jax.ShapeDtypeStruct((blocks, TILE_ROWS, cap * LAT_TILE), jnp.bfloat16),
        grid_spec=pltpu.PrefetchScalarGridSpec(
            num_scalar_prefetch=2,
            grid=(blocks,),
            in_specs=[
                pl.BlockSpec((TILE_ROWS, width), lambda b, i, n: (b, 0)),
                pl.BlockSpec((1, width), lambda b, i, n: (0, 0)),
            ]
            + [row_spec(c) for c in range(cap)]
            + [bias_spec(c) for c in range(cap)],
            out_specs=pl.BlockSpec((1, TILE_ROWS, cap * LAT_TILE), lambda b, i, n: (b, 0, 0)),
        ),
        compiler_params=pltpu.CompilerParams(vmem_limit_bytes=VMEM_BYTES),
        name="encode",
    )(ids, counts, gathered, dec_bias.reshape(1, -1), *([dictionary] * cap), *([bias] * cap))


def decode_kernel(cap, ids, place, codes_ref, *rest):
    w_refs, out_ref = rest[:cap], rest[cap]
    weights = jnp.concatenate([w[...] for w in w_refs], axis=0)
    part = jnp.dot(codes_ref[0], weights, preferred_element_type=jnp.float32)
    out_ref[...] = part.astype(jnp.bfloat16).reshape(out_ref.shape)


def decode(codes, ids, dictionary, tok_index, width, n_tok, n_lat):
    blocks, _, depth = codes.shape
    cap = depth // LAT_TILE
    per = blocks // n_tok
    rows = per * TILE_ROWS // n_lat
    split = TILE_ROWS // rows

    def row_spec(c):
        return pl.BlockSpec((LAT_TILE, width), lambda b, i, p: (i[b * cap + c], p[0]))

    return pl.pallas_call(
        functools.partial(decode_kernel, cap),
        out_shape=jax.ShapeDtypeStruct((n_lat, n_tok, rows, width), jnp.bfloat16),
        grid_spec=pltpu.PrefetchScalarGridSpec(
            num_scalar_prefetch=2,
            grid=(blocks,),
            in_specs=[pl.BlockSpec((1, TILE_ROWS, depth), lambda b, i, p: (b, 0, 0))]
            + [row_spec(c) for c in range(cap)],
            out_specs=pl.BlockSpec(
                (split, 1, rows, width), lambda b, i, p: (b % per, b // per, 0, 0)
            ),
        ),
        compiler_params=pltpu.CompilerParams(vmem_limit_bytes=VMEM_BYTES),
        name="decode",
    )(ids.reshape(-1), tok_index.reshape(1), codes, *([dictionary] * cap))


def grad_kernel(cap, per, ids, codes_ref, err_ref, out_ref):
    blocks = codes_ref.shape[0]
    split = TILE_ROWS // err_ref.shape[2]
    cols = err_ref.shape[3]
    out_ref[...] = jnp.zeros_like(out_ref)

    @pl.loop(0, blocks, unroll=4)
    def _(b):
        err = err_ref[pl.ds(lax.rem(b, per) * split, split), lax.div(b, per)]
        part = lax.dot_general(
            codes_ref[b],
            err.reshape(TILE_ROWS, cols),
            (((0,), (0,)), ((), ())),
            preferred_element_type=jnp.float32,
        )
        for c in range(cap):
            at = pl.ds(pl.multiple_of(ids[b * cap + c] * LAT_TILE, LAT_TILE), LAT_TILE)
            out_ref[at, :] += part[c * LAT_TILE : (c + 1) * LAT_TILE]


def grad(codes, ids, err, lat_rows):
    blocks, _, depth = codes.shape
    cap = depth // LAT_TILE
    n_lat, n_tok, rows, width = err.shape
    cols = 512
    return pl.pallas_call(
        functools.partial(grad_kernel, cap, blocks // n_tok),
        out_shape=jax.ShapeDtypeStruct((lat_rows, width), jnp.float32),
        grid_spec=pltpu.PrefetchScalarGridSpec(
            num_scalar_prefetch=1,
            grid=(width // cols,),
            in_specs=[
                pl.BlockSpec(codes.shape, lambda j, i: (0, 0, 0)),
                pl.BlockSpec((n_lat, n_tok, rows, cols), lambda j, i: (0, 0, 0, j)),
            ],
            out_specs=pl.BlockSpec((lat_rows, cols), lambda j, i: (0, j)),
        ),
        compiler_params=pltpu.CompilerParams(vmem_limit_bytes=VMEM_BYTES),
        name="grad",
    )(ids.reshape(-1), codes, err)


def body(residuals, dictionary, enc_bias, dec_bias, tile_ids, tile_counts):
    n_tok, n_lat = lax.axis_size("tok"), lax.axis_size("lat")
    tok_index, lat_index = lax.axis_index("tok"), lax.axis_index("lat")
    tok_rows = residuals.shape[0]
    blocks, _, cap = tile_ids.shape
    width = dictionary.shape[1] // n_tok
    rows = tok_rows // n_lat
    ids = tile_ids[:, 0, :]
    ids_all = lax.all_gather(tile_ids[:, 0, :], "tok", axis=0, tiled=True).reshape(-1)
    gathered = lax.all_gather(residuals, "lat", axis=1, tiled=True)
    codes = encode(gathered, dictionary, enc_bias, dec_bias, ids, tile_counts[:, 0])
    codes_all = lax.all_gather(codes, "tok", axis=0, tiled=True)
    partial_sum = decode(codes_all, ids_all, dictionary, tok_index, width, n_tok, n_lat)
    own_rows = lax.dynamic_slice_in_dim(gathered, lat_index * rows, rows, 0)
    share = lax.all_to_all(
        own_rows.reshape(rows, n_tok, width).transpose(1, 0, 2), "tok", 0, 0, tiled=True
    )
    summed = lax.psum_scatter(partial_sum, "lat", scatter_dimension=0, tiled=False)
    bias = lax.dynamic_slice_in_dim(dec_bias, tok_index * width, width, 0)
    recon = summed.astype(jnp.float32) + bias
    err = (recon - share.astype(jnp.float32)).astype(jnp.bfloat16)
    err_all = lax.all_gather(err, "lat", axis=0, tiled=False)
    decoder_grad = grad(codes_all, ids_all, err_all, dictionary.shape[0])
    back = lax.all_to_all(recon.astype(jnp.bfloat16), "tok", 0, 0, tiled=True)
    back = back.transpose(1, 0, 2).reshape(rows, n_lat, -1).transpose(1, 0, 2)
    reconstruction = lax.all_to_all(back, "lat", 0, 0, tiled=True).reshape(tok_rows, -1)
    sent = codes.reshape(blocks, n_lat, TILE_ROWS // n_lat, cap, LAT_TILE)
    sent = sent.transpose(1, 0, 3, 2, 4).reshape(n_lat, blocks, cap, -1)
    tile_codes = lax.all_to_all(sent, "lat", 0, 0, tiled=True).transpose(1, 0, 2, 3)
    return (tile_codes, reconstruction, decoder_grad)


def step_kernel(
    cap,
    res_ref, rows_hbm, cols_hbm, enc_ref, dec_ref, live_ref,
    codes_ref, err_ref, tc_ref, rec_ref,
    rows_v, cols_v, gath, mine, sib_out, sib_in, fwd_x, fwd_y, dir_x, dir_y, sum_x, sum_y,
    share, rec, rows_full,
    rows_sem, cols_sem, g_send, g_recv, e_send, e_recv,
    c_send, c_recv, h_send, h_recv, t_send, t_recv, s_send, s_recv, p_send, p_recv,
    b_send, b_recv, r_send, r_recv,
):
    z, lat = lax.axis_index("tok"), lax.axis_index("lat")
    core, chip = lax.rem(lat, 2), lax.div(lat, 2)
    x, y = lax.rem(chip, 2), lax.div(chip, 2)

    def flip(m):
        yy = 1 - y if m & 4 else y
        xx = 1 - x if m & 2 else x
        cc = 1 - core if m & 1 else core
        return (yy * 2 + xx) * 2 + cc

    started = []

    def send(src, dst, send_sem, recv_sem, **where):
        copy = pltpu.make_async_remote_copy(
            src_ref=src, dst_ref=dst, send_sem=send_sem, recv_sem=recv_sem,
            device_id=where, device_id_type=pl.DeviceIdType.MESH,
        )
        copy.start()
        started.append(copy)

    def arrive(dst, send_sem, recv_sem):
        pltpu.make_async_remote_copy(
            src_ref=dst, dst_ref=dst, send_sem=send_sem, recv_sem=recv_sem,
            device_id={"lat": flip(1)}, device_id_type=pl.DeviceIdType.MESH,
        ).wait_recv()

    load_rows = pltpu.make_async_copy(rows_hbm, rows_v, rows_sem)
    load_rows.start()
    load_cols = pltpu.make_async_copy(cols_hbm, cols_v, cols_sem)
    load_cols.start()
    barrier = pltpu.get_barrier_semaphore()
    for m in range(1, 8):
        pl.semaphore_signal(
            barrier, inc=1, device_id={"lat": flip(m)}, device_id_type=pl.DeviceIdType.MESH
        )
    for d in range(1, 4):
        pl.semaphore_signal(
            barrier, inc=1, device_id={"tok": lax.rem(z + d, 4)},
            device_id_type=pl.DeviceIdType.MESH,
        )
    pl.semaphore_wait(barrier, 10)

    def gather_start(ref, own, i, ss, rs):
        send(own, ref.at[lat, i], ss.at[i, 0], rs.at[i, 2], lat=flip(2))
        send(own, ref.at[lat, i], ss.at[i, 1], rs.at[i, 4], lat=flip(4))
        send(own, ref.at[lat, i], ss.at[i, 2], rs.at[i, 1], lat=flip(1))

    def gather_near(ref, i, ss, rs):
        at_x, at_y = ref.at[flip(2), i], ref.at[flip(4), i]
        arrive(at_x, ss.at[i, 0], rs.at[i, 2])
        if i % 2 == 0:
            send(at_x, at_x, ss.at[i, 3], rs.at[i, 6], lat=flip(4))
        send(at_x, at_x, ss.at[i, 4], rs.at[i, 3], lat=flip(1))
        arrive(at_y, ss.at[i, 0], rs.at[i, 4])
        if i % 2 == 1:
            send(at_y, at_y, ss.at[i, 3], rs.at[i, 6], lat=flip(2))
        send(at_y, at_y, ss.at[i, 5], rs.at[i, 5], lat=flip(1))

    def gather_far(ref, i, ss, rs):
        at_d = ref.at[flip(6), i]
        arrive(at_d, ss.at[i, 0], rs.at[i, 6])
        send(at_d, at_d, ss.at[i, 6], rs.at[i, 7], lat=flip(1))

    def gather_end(ref, i, ss, rs):
        for m in (1, 3, 5, 7):
            arrive(ref.at[flip(m), i], ss.at[i, 0], rs.at[i, m])

    for i in range(4):
        gather_start(gath, res_ref.at[i], i, g_send, g_recv)
    for i in range(4):
        gath[lat, i] = res_ref[i]
    gather_near(gath, 0, g_send, g_recv)
    load_rows.wait()

    for i in range(4):
        if i < 3:
            gather_near(gath, i + 1, g_send, g_recv)
        gather_far(gath, i, g_send, g_recv)
        gather_end(gath, i, g_send, g_recv)
        preact = enc_ref[i]
        for s in range(8):
            centered = (gath[s, i].astype(jnp.float32) - dec_ref[s]).astype(jnp.bfloat16)
            weights = rows_v[i, :, s * 512 : (s + 1) * 512]
            preact = preact + lax.dot_general(
                centered, weights, (((1,), (1,)), ((), ())), preferred_element_type=jnp.float32
            )
        codes_ref[z * 4 + i] = (jnp.maximum(preact, 0.0) * live_ref[i]).astype(jnp.bfloat16)
        for d in range(1, 4):
            block = codes_ref.at[z * 4 + i]
            send(block, block, c_send.at[i, d], c_recv.at[i, d], tok=lax.rem(z + d, 4))

    own_rows = pl.ds(pl.multiple_of(core * 64, 64), 64)
    other_rows = pl.ds(pl.multiple_of((1 - core) * 64, 64), 64)
    for d in range(1, 4):
        to = lax.rem(z + d, 4)
        send(
            gath.at[pl.ds(to * 2, 2), chip, own_rows], share.at[z],
            h_send.at[d], h_recv.at[d], tok=to,
        )
    for h in range(2):
        share[z, h] = gath[z * 2 + h, chip, own_rows]

    for i in range(4):
        for d in range(1, 4):
            src = lax.rem(z + 4 - d, 4)
            arrive(codes_ref.at[src * 4 + i], c_send.at[i, d], c_recv.at[i, d])

    load_cols.wait()
    for r, m in enumerate((6, 2, 4, 0)):
        to_chip = lax.div(flip(m), 2)

        @pl.loop(0, 4)
        def _(q):
            block = q * 4 + to_chip
            weights = cols_v[block]
            sib_out[r, q] = jnp.dot(
                codes_ref[block, other_rows, :], weights, preferred_element_type=jnp.float32
            ).astype(jnp.bfloat16)
            mine[r, q] = jnp.dot(
                codes_ref[block, own_rows, :], weights, preferred_element_type=jnp.float32
            ).astype(jnp.bfloat16)

        send(sib_out.at[r], sib_in.at[r], s_send.at[r], s_recv.at[r], lat=flip(1))

    def add(r, q, *more):
        total = mine[r, q].astype(jnp.float32) + sib_in[r, q].astype(jnp.float32)
        for ref in more:
            total = total + ref.astype(jnp.float32)
        return total

    def settle(r, q, *more):
        mine[r, q] = add(r, q, *more).astype(jnp.bfloat16)

    first, second = pl.ds(0, 2), pl.ds(2, 2)
    arrive(sib_in.at[0], s_send.at[0], s_recv.at[0])
    for q in range(4):
        settle(0, q)
    send(mine.at[0, first], fwd_x, p_send.at[0], p_recv.at[0], lat=flip(2))
    send(mine.at[0, second], fwd_y, p_send.at[1], p_recv.at[1], lat=flip(4))
    arrive(sib_in.at[1], s_send.at[1], s_recv.at[1])
    for q in range(2):
        settle(1, q)
    send(mine.at[1, first], dir_x, p_send.at[2], p_recv.at[2], lat=flip(2))
    arrive(sib_in.at[2], s_send.at[2], s_recv.at[2])
    for q in range(2, 4):
        settle(2, q)
    send(mine.at[2, second], dir_y, p_send.at[3], p_recv.at[3], lat=flip(4))
    arrive(fwd_x, p_send.at[0], p_recv.at[0])
    for q in range(2):
        settle(2, q, fwd_x[q])
    send(mine.at[2, first], sum_y, p_send.at[4], p_recv.at[4], lat=flip(4))
    arrive(fwd_y, p_send.at[1], p_recv.at[1])
    for q in range(2, 4):
        settle(1, q, fwd_y[q - 2])
    send(mine.at[1, second], sum_x, p_send.at[5], p_recv.at[5], lat=flip(2))
    arrive(sib_in.at[3], s_send.at[3], s_recv.at[3])
    for d in range(1, 4):
        arrive(share.at[lax.rem(z + 4 - d, 4)], h_send.at[d], h_recv.at[d])

    bias = jnp.concatenate([dec_ref[z * 2], dec_ref[z * 2 + 1]], axis=1)

    def finish(q, *more):
        recon = add(3, q, *more) + bias
        rec[q] = recon.astype(jnp.bfloat16)
        res = jnp.concatenate([share[q, 0], share[q, 1]], axis=1).astype(jnp.float32)
        err_ref[lat, q] = (recon - res).astype(jnp.bfloat16)
        gather_start(err_ref, err_ref.at[lat, q], q, e_send, e_recv)

    arrive(dir_x, p_send.at[2], p_recv.at[2])
    arrive(sum_y, p_send.at[4], p_recv.at[4])
    for q in range(2):
        finish(q, dir_x[q], sum_y[q])
    arrive(dir_y, p_send.at[3], p_recv.at[3])
    arrive(sum_x, p_send.at[5], p_recv.at[5])
    for q in range(2, 4):
        finish(q, dir_y[q - 2], sum_x[q - 2])

    for d in range(1, 4):
        to = lax.rem(z + d, 4)
        send(rec.at[to], rows_full.at[z], b_send.at[d], b_recv.at[d], tok=to)
    rows_full[z] = rec[z]
    gather_near(err_ref, 0, e_send, e_recv)
    gather_near(err_ref, 1, e_send, e_recv)
    for i in range(4):
        if i < 2:
            gather_near(err_ref, i + 2, e_send, e_recv)
        gather_far(err_ref, i, e_send, e_recv)

    own_blocks = pl.ds(z * 4, 4)

    def code_rows(owner):
        return pl.ds(pl.multiple_of(owner * 16, 16), 16)

    for m in range(1, 8):
        to = flip(m)
        send(
            codes_ref.at[own_blocks, code_rows(to), :], tc_ref.at[lat],
            t_send.at[m], t_recv.at[m], lat=to,
        )
    tc_ref[lat] = codes_ref[own_blocks, code_rows(lat), :]
    for d in range(1, 4):
        src = lax.rem(z + 4 - d, 4)
        arrive(rows_full.at[src], b_send.at[d], b_recv.at[d])

    def columns(owner):
        return pl.ds(pl.multiple_of(lax.rem(owner, 2) * 512, 512), 512)

    for m in range(1, 8):
        to = flip(m)
        send(
            rows_full.at[lax.div(to, 2), :, columns(to)], rec_ref.at[lat],
            r_send.at[m], r_recv.at[m], lat=to,
        )
    rec_ref[lat] = rows_full[chip, :, columns(lat)]
    for i in range(4):
        gather_end(err_ref, i, e_send, e_recv)
    for m in range(1, 8):
        arrive(tc_ref.at[flip(m)], t_send.at[m], t_recv.at[m])
        arrive(rec_ref.at[flip(m)], r_send.at[m], r_recv.at[m])
    for copy in started:
        copy.wait_send()


def select_kernel(ids, place, *refs):
    out_ref = refs[-1]
    for n, ref in enumerate(refs[:-1]):
        at = (n * LAT_TILE) % out_ref.shape[1]
        out_ref[n * LAT_TILE // out_ref.shape[1], at : at + LAT_TILE] = ref[...]


def select(ids, place, dictionary, cap, group, width):
    blocks, depth = ids.size // cap, cap * LAT_TILE

    def row_spec(n):
        return pl.BlockSpec((LAT_TILE, width), lambda b, i, p: (i[b * group * cap + n], p[0]))

    return pl.pallas_call(
        select_kernel,
        out_shape=jax.ShapeDtypeStruct((blocks, depth, width), jnp.bfloat16),
        grid_spec=pltpu.PrefetchScalarGridSpec(
            num_scalar_prefetch=2,
            grid=(blocks // group,),
            in_specs=[row_spec(n) for n in range(group * cap)],
            out_specs=pl.BlockSpec((group, depth, width), lambda b, i, p: (b, 0, 0)),
        ),
        compiler_params=pltpu.CompilerParams(vmem_limit_bytes=VMEM_BYTES),
        cost_estimate=pl.CostEstimate(
            flops=0, bytes_accessed=4 * blocks * depth * width, transcendentals=0
        ),
        name="select",
    )(ids, place.reshape(1), *([dictionary] * (group * cap)))


def small_body(residuals, dictionary, enc_bias, dec_bias, tile_ids, tile_counts):
    cap = tile_ids.shape[2]
    lat_rows, model = dictionary.shape
    ids = tile_ids.reshape(-1)
    pieces = [ids] + [
        lax.ppermute(ids, "tok", [(n, (n + d) % 4) for n in range(4)]) for d in range(1, 4)
    ]
    group = jnp.arange(4, dtype=jnp.int32)[:, None]
    from_group = lax.rem(lax.axis_index("tok") + 4 - group, 4)
    ids_all = sum(jnp.where(from_group == d, pieces[d][None, :], 0) for d in range(4)).reshape(-1)
    rows_sel = select(ids, jnp.zeros((), jnp.int32), dictionary, cap, 1, model)
    cols_sel = select(ids_all, lax.axis_index("tok"), dictionary, cap, 2, 1024)
    bias = enc_bias.reshape(-1, LAT_TILE)[ids].reshape(4, 1, cap * LAT_TILE)
    live = jnp.arange(cap, dtype=jnp.int32)[None, :] < tile_counts
    live = jnp.repeat(live.astype(jnp.float32), LAT_TILE, axis=1).reshape(4, 1, cap * LAT_TILE)
    bf16, f32, dma = jnp.bfloat16, jnp.float32, pltpu.SemaphoreType.DMA
    vmem, anywhere = pl.BlockSpec(memory_space=pltpu.VMEM), pl.BlockSpec(memory_space=pl.ANY)
    codes_all, err_all, tiles, recon = pl.pallas_call(
        functools.partial(step_kernel, cap),
        out_shape=[
            jax.ShapeDtypeStruct((16, 128, cap * LAT_TILE), bf16),
            jax.ShapeDtypeStruct((8, 4, 64, 1024), bf16),
            jax.ShapeDtypeStruct((8, 4, 16, cap * LAT_TILE), bf16),
            jax.ShapeDtypeStruct((8, 64, 512), bf16),
        ],
        in_specs=[vmem, anywhere, anywhere, vmem, vmem, vmem],
        out_specs=[vmem, vmem, vmem, vmem],
        scratch_shapes=[
            pltpu.VMEM(rows_sel.shape, bf16),
            pltpu.VMEM(cols_sel.shape, bf16),
            pltpu.VMEM((8, 4, 128, 512), bf16),
            pltpu.VMEM((4, 4, 64, 1024), bf16),
            pltpu.VMEM((4, 4, 64, 1024), bf16),
            pltpu.VMEM((4, 4, 64, 1024), bf16),
        ]
        + [pltpu.VMEM((2, 64, 1024), bf16)] * 6
        + [
            pltpu.VMEM((4, 2, 64, 512), bf16),
            pltpu.VMEM((4, 64, 1024), bf16),
            pltpu.VMEM((4, 64, 1024), bf16),
            dma, dma,
            dma((4, 7)), dma((4, 8)), dma((4, 7)), dma((4, 8)),
            dma((4, 4)), dma((4, 4)),
            dma((4,)), dma((4,)),
            dma((8,)), dma((8,)),
            dma((4,)), dma((4,)),
            dma((6,)), dma((6,)),
            dma((4,)), dma((4,)),
            dma((8,)), dma((8,)),
        ],
        compiler_params=pltpu.CompilerParams(
            collective_id=0, has_side_effects=True, vmem_limit_bytes=VMEM_BYTES
        ),
        name="step",
    )(
        residuals.reshape(4, 128, 512),
        rows_sel,
        cols_sel,
        bias,
        dec_bias.reshape(8, 1, 512),
        live,
    )
    decoder_grad = grad(codes_all, ids_all, err_all, lat_rows)
    tiles = tiles.reshape(8, 4, 16, cap, LAT_TILE).transpose(1, 0, 3, 2, 4).reshape(4, 8, cap, -1)
    return tiles, recon.reshape(512, 512), decoder_grad


def solution(mesh):
    sizes = dict(mesh.shape)
    chosen = small_body if sizes == {"tok": 4, "lat": 8} else body
    placed = (
        P("tok", "lat"),
        P("lat", None),
        P("lat"),
        P(),
        P("tok", "lat", None),
        P("tok", "lat"),
    )
    return jax.shard_map(
        chosen,
        mesh=mesh,
        in_specs=placed,
        out_specs=(P("tok", None, None, "lat"), P("tok", "lat"), P("lat", "tok")),
        check_vma=False,
    )
```

```python
import functools

import jax
import jax.numpy as jnp
from jax import lax
from jax.experimental import pallas as pl
from jax.experimental.pallas import tpu as pltpu
from jax.sharding import PartitionSpec as P

TILE_ROWS = 128
LAT_TILE = 64
VMEM_BYTES = 48 * 1024 * 1024


def encode_kernel(cap, ids, counts, res_ref, dec_ref, *rest):
    w_refs, e_refs, out_ref = rest[:cap], rest[cap : 2 * cap], rest[2 * cap]
    b = pl.program_id(0)
    centered = (res_ref[...].astype(jnp.float32) - dec_ref[...]).astype(jnp.bfloat16)
    weights = jnp.concatenate([w[...] for w in w_refs], axis=0)
    preact = lax.dot_general(
        centered, weights, (((1,), (1,)), ((), ())), preferred_element_type=jnp.float32
    )
    bias = jnp.concatenate([e[0] for e in e_refs], axis=1)
    slot = lax.broadcasted_iota(jnp.int32, (1, cap * LAT_TILE), 1) // LAT_TILE
    live = (slot < counts[b]).astype(jnp.float32)
    out_ref[0] = (jnp.maximum(preact + bias, 0.0) * live).astype(jnp.bfloat16)


def encode(gathered, dictionary, enc_bias, dec_bias, ids, counts):
    tok_rows, width = gathered.shape
    blocks, cap = ids.shape
    lat_blocks = dictionary.shape[0] // LAT_TILE
    ids = ids.reshape(-1)
    bias = enc_bias.reshape(lat_blocks, 1, LAT_TILE)

    def row_spec(c):
        return pl.BlockSpec((LAT_TILE, width), lambda b, i, n: (i[b * cap + c], 0))

    def bias_spec(c):
        return pl.BlockSpec((1, 1, LAT_TILE), lambda b, i, n: (i[b * cap + c], 0, 0))

    return pl.pallas_call(
        functools.partial(encode_kernel, cap),
        out_shape=jax.ShapeDtypeStruct((blocks, TILE_ROWS, cap * LAT_TILE), jnp.bfloat16),
        grid_spec=pltpu.PrefetchScalarGridSpec(
            num_scalar_prefetch=2,
            grid=(blocks,),
            in_specs=[
                pl.BlockSpec((TILE_ROWS, width), lambda b, i, n: (b, 0)),
                pl.BlockSpec((1, width), lambda b, i, n: (0, 0)),
            ]
            + [row_spec(c) for c in range(cap)]
            + [bias_spec(c) for c in range(cap)],
            out_specs=pl.BlockSpec((1, TILE_ROWS, cap * LAT_TILE), lambda b, i, n: (b, 0, 0)),
        ),
        compiler_params=pltpu.CompilerParams(vmem_limit_bytes=VMEM_BYTES),
        name="encode",
    )(ids, counts, gathered, dec_bias.reshape(1, -1), *([dictionary] * cap), *([bias] * cap))


def decode_kernel(cap, ids, place, codes_ref, *rest):
    w_refs, out_ref = rest[:cap], rest[cap]
    weights = jnp.concatenate([w[...] for w in w_refs], axis=0)
    part = jnp.dot(codes_ref[0], weights, preferred_element_type=jnp.float32)
    out_ref[...] = part.astype(jnp.bfloat16).reshape(out_ref.shape)


def decode(codes, ids, dictionary, tok_index, width, n_tok, n_lat):
    blocks, _, depth = codes.shape
    cap = depth // LAT_TILE
    per = blocks // n_tok
    rows = per * TILE_ROWS // n_lat
    split = TILE_ROWS // rows

    def row_spec(c):
        return pl.BlockSpec((LAT_TILE, width), lambda b, i, p: (i[b * cap + c], p[0]))

    return pl.pallas_call(
        functools.partial(decode_kernel, cap),
        out_shape=jax.ShapeDtypeStruct((n_lat, n_tok, rows, width), jnp.bfloat16),
        grid_spec=pltpu.PrefetchScalarGridSpec(
            num_scalar_prefetch=2,
            grid=(blocks,),
            in_specs=[pl.BlockSpec((1, TILE_ROWS, depth), lambda b, i, p: (b, 0, 0))]
            + [row_spec(c) for c in range(cap)],
            out_specs=pl.BlockSpec(
                (split, 1, rows, width), lambda b, i, p: (b % per, b // per, 0, 0)
            ),
        ),
        compiler_params=pltpu.CompilerParams(vmem_limit_bytes=VMEM_BYTES),
        name="decode",
    )(ids.reshape(-1), tok_index.reshape(1), codes, *([dictionary] * cap))


def grad_kernel(cap, per, ids, codes_ref, err_ref, out_ref):
    blocks = codes_ref.shape[0]
    split = TILE_ROWS // err_ref.shape[2]
    cols = err_ref.shape[3]
    out_ref[...] = jnp.zeros_like(out_ref)

    @pl.loop(0, blocks, unroll=4)
    def _(b):
        err = err_ref[pl.ds(lax.rem(b, per) * split, split), lax.div(b, per)]
        part = lax.dot_general(
            codes_ref[b],
            err.reshape(TILE_ROWS, cols),
            (((0,), (0,)), ((), ())),
            preferred_element_type=jnp.float32,
        )
        for c in range(cap):
            at = pl.ds(pl.multiple_of(ids[b * cap + c] * LAT_TILE, LAT_TILE), LAT_TILE)
            out_ref[at, :] += part[c * LAT_TILE : (c + 1) * LAT_TILE]


def grad(codes, ids, err, lat_rows):
    blocks, _, depth = codes.shape
    cap = depth // LAT_TILE
    n_lat, n_tok, rows, width = err.shape
    cols = 512
    return pl.pallas_call(
        functools.partial(grad_kernel, cap, blocks // n_tok),
        out_shape=jax.ShapeDtypeStruct((lat_rows, width), jnp.float32),
        grid_spec=pltpu.PrefetchScalarGridSpec(
            num_scalar_prefetch=1,
            grid=(width // cols,),
            in_specs=[
                pl.BlockSpec(codes.shape, lambda j, i: (0, 0, 0)),
                pl.BlockSpec((n_lat, n_tok, rows, cols), lambda j, i: (0, 0, 0, j)),
            ],
            out_specs=pl.BlockSpec((lat_rows, cols), lambda j, i: (0, j)),
        ),
        compiler_params=pltpu.CompilerParams(vmem_limit_bytes=VMEM_BYTES),
        name="grad",
    )(ids.reshape(-1), codes, err)


def body(residuals, dictionary, enc_bias, dec_bias, tile_ids, tile_counts):
    n_tok, n_lat = lax.axis_size("tok"), lax.axis_size("lat")
    tok_index, lat_index = lax.axis_index("tok"), lax.axis_index("lat")
    tok_rows = residuals.shape[0]
    blocks, _, cap = tile_ids.shape
    width = dictionary.shape[1] // n_tok
    rows = tok_rows // n_lat
    ids = tile_ids[:, 0, :]
    ids_all = lax.all_gather(tile_ids[:, 0, :], "tok", axis=0, tiled=True).reshape(-1)
    gathered = lax.all_gather(residuals, "lat", axis=1, tiled=True)
    codes = encode(gathered, dictionary, enc_bias, dec_bias, ids, tile_counts[:, 0])
    codes_all = lax.all_gather(codes, "tok", axis=0, tiled=True)
    partial_sum = decode(codes_all, ids_all, dictionary, tok_index, width, n_tok, n_lat)
    own_rows = lax.dynamic_slice_in_dim(gathered, lat_index * rows, rows, 0)
    share = lax.all_to_all(
        own_rows.reshape(rows, n_tok, width).transpose(1, 0, 2), "tok", 0, 0, tiled=True
    )
    summed = lax.psum_scatter(partial_sum, "lat", scatter_dimension=0, tiled=False)
    bias = lax.dynamic_slice_in_dim(dec_bias, tok_index * width, width, 0)
    recon = summed.astype(jnp.float32) + bias
    err = (recon - share.astype(jnp.float32)).astype(jnp.bfloat16)
    err_all = lax.all_gather(err, "lat", axis=0, tiled=False)
    decoder_grad = grad(codes_all, ids_all, err_all, dictionary.shape[0])
    back = lax.all_to_all(recon.astype(jnp.bfloat16), "tok", 0, 0, tiled=True)
    back = back.transpose(1, 0, 2).reshape(rows, n_lat, -1).transpose(1, 0, 2)
    reconstruction = lax.all_to_all(back, "lat", 0, 0, tiled=True).reshape(tok_rows, -1)
    sent = codes.reshape(blocks, n_lat, TILE_ROWS // n_lat, cap, LAT_TILE)
    sent = sent.transpose(1, 0, 3, 2, 4).reshape(n_lat, blocks, cap, -1)
    tile_codes = lax.all_to_all(sent, "lat", 0, 0, tiled=True).transpose(1, 0, 2, 3)
    return (tile_codes, reconstruction, decoder_grad)


def step_kernel(
    cap,
    res_ref, rows_hbm, cols_hbm, enc_ref, dec_ref, live_ref,
    codes_ref, err_ref, tc_ref, rec_ref,
    rows_v, cols_v, gath, mine, sib_in, fwd_x, fwd_y, dir_x, dir_y, sum_x, sum_y,
    share, rec, rows_full,
    rows_sem, cols_sem, g_send, g_recv, e_send, e_recv,
    c_send, c_recv, h_send, h_recv, t_send, t_recv, s_send, s_recv, p_send, p_recv,
    b_send, b_recv, r_send, r_recv,
):
    z, lat = lax.axis_index("tok"), lax.axis_index("lat")
    core, chip = lax.rem(lat, 2), lax.div(lat, 2)
    x, y = lax.rem(chip, 2), lax.div(chip, 2)

    def flip(m):
        yy = 1 - y if m & 4 else y
        xx = 1 - x if m & 2 else x
        cc = 1 - core if m & 1 else core
        return (yy * 2 + xx) * 2 + cc

    started = []

    def send(src, dst, send_sem, recv_sem, **where):
        copy = pltpu.make_async_remote_copy(
            src_ref=src, dst_ref=dst, send_sem=send_sem, recv_sem=recv_sem,
            device_id=where, device_id_type=pl.DeviceIdType.MESH,
        )
        copy.start()
        started.append(copy)

    def arrive(dst, send_sem, recv_sem):
        pltpu.make_async_remote_copy(
            src_ref=dst, dst_ref=dst, send_sem=send_sem, recv_sem=recv_sem,
            device_id={"lat": flip(1)}, device_id_type=pl.DeviceIdType.MESH,
        ).wait_recv()

    load_rows = pltpu.make_async_copy(rows_hbm, rows_v, rows_sem)
    load_rows.start()
    load_cols = pltpu.make_async_copy(cols_hbm, cols_v, cols_sem)
    load_cols.start()
    barrier = pltpu.get_barrier_semaphore()
    for m in range(1, 8):
        pl.semaphore_signal(
            barrier, inc=1, device_id={"lat": flip(m)}, device_id_type=pl.DeviceIdType.MESH
        )
    for d in range(1, 4):
        pl.semaphore_signal(
            barrier, inc=1, device_id={"tok": lax.rem(z + d, 4)},
            device_id_type=pl.DeviceIdType.MESH,
        )
    pl.semaphore_wait(barrier, 10)

    def gather_start(ref, own, i, ss, rs):
        send(own, ref.at[lat, i], ss.at[i, 0], rs.at[i, 2], lat=flip(2))
        send(own, ref.at[lat, i], ss.at[i, 1], rs.at[i, 4], lat=flip(4))
        send(own, ref.at[lat, i], ss.at[i, 2], rs.at[i, 1], lat=flip(1))

    def gather_near(ref, i, ss, rs):
        at_x, at_y = ref.at[flip(2), i], ref.at[flip(4), i]
        arrive(at_x, ss.at[i, 0], rs.at[i, 2])
        if i % 2 == 0:
            send(at_x, at_x, ss.at[i, 3], rs.at[i, 6], lat=flip(4))
        send(at_x, at_x, ss.at[i, 4], rs.at[i, 3], lat=flip(1))
        arrive(at_y, ss.at[i, 0], rs.at[i, 4])
        if i % 2 == 1:
            send(at_y, at_y, ss.at[i, 3], rs.at[i, 6], lat=flip(2))
        send(at_y, at_y, ss.at[i, 5], rs.at[i, 5], lat=flip(1))

    def gather_far(ref, i, ss, rs):
        at_d = ref.at[flip(6), i]
        arrive(at_d, ss.at[i, 0], rs.at[i, 6])
        send(at_d, at_d, ss.at[i, 6], rs.at[i, 7], lat=flip(1))

    def gather_end(ref, i, ss, rs):
        for m in (1, 3, 5, 7):
            arrive(ref.at[flip(m), i], ss.at[i, 0], rs.at[i, m])

    for i in range(4):
        gather_start(gath, res_ref.at[i], i, g_send, g_recv)
    for i in range(4):
        gath[lat, i] = res_ref[i]
    gather_near(gath, 0, g_send, g_recv)
    load_rows.wait()

    for i in range(4):
        if i < 3:
            gather_near(gath, i + 1, g_send, g_recv)
        gather_far(gath, i, g_send, g_recv)
        gather_end(gath, i, g_send, g_recv)
        preact = enc_ref[i]
        for s in range(8):
            centered = (gath[s, i].astype(jnp.float32) - dec_ref[s]).astype(jnp.bfloat16)
            weights = rows_v[i, :, s * 512 : (s + 1) * 512]
            preact = preact + lax.dot_general(
                centered, weights, (((1,), (1,)), ((), ())), preferred_element_type=jnp.float32
            )
        codes_ref[z * 4 + i] = (jnp.maximum(preact, 0.0) * live_ref[i]).astype(jnp.bfloat16)
        for d in range(1, 4):
            block = codes_ref.at[z * 4 + i]
            send(block, block, c_send.at[i, d], c_recv.at[i, d], tok=lax.rem(z + d, 4))

    own_rows = pl.ds(pl.multiple_of(core * 64, 64), 64)
    other_rows = pl.ds(pl.multiple_of((1 - core) * 64, 64), 64)
    for d in range(1, 4):
        to = lax.rem(z + d, 4)
        send(
            gath.at[pl.ds(to * 2, 2), chip, own_rows], share.at[z],
            h_send.at[d], h_recv.at[d], tok=to,
        )
    for h in range(2):
        share[z, h] = gath[z * 2 + h, chip, own_rows]

    for i in range(4):
        for d in range(1, 4):
            src = lax.rem(z + 4 - d, 4)
            arrive(codes_ref.at[src * 4 + i], c_send.at[i, d], c_recv.at[i, d])

    own_blocks = pl.ds(z * 4, 4)

    def code_rows(owner):
        return pl.ds(pl.multiple_of(owner * 16, 16), 16)

    for m in range(1, 8):
        to = flip(m)
        send(
            codes_ref.at[own_blocks, code_rows(to), :], tc_ref.at[lat],
            t_send.at[m], t_recv.at[m], lat=to,
        )
    tc_ref[lat] = codes_ref[own_blocks, code_rows(lat), :]
    load_cols.wait()
    for r, m in enumerate((6, 2, 4, 0)):
        to_chip = lax.div(flip(m), 2)

        @pl.loop(0, 4)
        def _(q):
            block = q * 4 + to_chip
            weights = cols_v[block]
            mine[r, q] = jnp.dot(
                codes_ref[block], weights, preferred_element_type=jnp.float32
            ).astype(jnp.bfloat16)

        send(mine.at[r, :, other_rows], sib_in.at[r], s_send.at[r], s_recv.at[r], lat=flip(1))

    def add(r, q, *more):
        total = mine[r, q, own_rows, :].astype(jnp.float32) + sib_in[r, q].astype(jnp.float32)
        for ref in more:
            total = total + ref.astype(jnp.float32)
        return total

    def settle(r, q, *more):
        mine[r, q, own_rows, :] = add(r, q, *more).astype(jnp.bfloat16)

    first, second = pl.ds(0, 2), pl.ds(2, 2)
    arrive(sib_in.at[0], s_send.at[0], s_recv.at[0])
    for q in range(4):
        settle(0, q)
    send(mine.at[0, first, own_rows], fwd_x, p_send.at[0], p_recv.at[0], lat=flip(2))
    send(mine.at[0, second, own_rows], fwd_y, p_send.at[1], p_recv.at[1], lat=flip(4))
    arrive(sib_in.at[1], s_send.at[1], s_recv.at[1])
    for q in range(2):
        settle(1, q)
    send(mine.at[1, first, own_rows], dir_x, p_send.at[2], p_recv.at[2], lat=flip(2))
    arrive(sib_in.at[2], s_send.at[2], s_recv.at[2])
    for q in range(2, 4):
        settle(2, q)
    send(mine.at[2, second, own_rows], dir_y, p_send.at[3], p_recv.at[3], lat=flip(4))
    arrive(fwd_x, p_send.at[0], p_recv.at[0])
    for q in range(2):
        settle(2, q, fwd_x[q])
    send(mine.at[2, first, own_rows], sum_y, p_send.at[4], p_recv.at[4], lat=flip(4))
    arrive(fwd_y, p_send.at[1], p_recv.at[1])
    for q in range(2, 4):
        settle(1, q, fwd_y[q - 2])
    send(mine.at[1, second, own_rows], sum_x, p_send.at[5], p_recv.at[5], lat=flip(2))
    arrive(sib_in.at[3], s_send.at[3], s_recv.at[3])
    for d in range(1, 4):
        arrive(share.at[lax.rem(z + 4 - d, 4)], h_send.at[d], h_recv.at[d])

    bias = jnp.concatenate([dec_ref[z * 2], dec_ref[z * 2 + 1]], axis=1)

    def finish(q, *more):
        recon = add(3, q, *more) + bias
        rec[q] = recon.astype(jnp.bfloat16)
        res = jnp.concatenate([share[q, 0], share[q, 1]], axis=1).astype(jnp.float32)
        err_ref[lat, q] = (recon - res).astype(jnp.bfloat16)
        gather_start(err_ref, err_ref.at[lat, q], q, e_send, e_recv)

    arrive(dir_x, p_send.at[2], p_recv.at[2])
    arrive(sum_y, p_send.at[4], p_recv.at[4])
    for q in range(2):
        finish(q, dir_x[q], sum_y[q])
    arrive(dir_y, p_send.at[3], p_recv.at[3])
    arrive(sum_x, p_send.at[5], p_recv.at[5])
    for q in range(2, 4):
        finish(q, dir_y[q - 2], sum_x[q - 2])

    for d in range(1, 4):
        to = lax.rem(z + d, 4)
        send(rec.at[to], rows_full.at[z], b_send.at[d], b_recv.at[d], tok=to)
    rows_full[z] = rec[z]
    gather_near(err_ref, 0, e_send, e_recv)
    gather_near(err_ref, 1, e_send, e_recv)
    for i in range(4):
        if i < 2:
            gather_near(err_ref, i + 2, e_send, e_recv)
        gather_far(err_ref, i, e_send, e_recv)

    for d in range(1, 4):
        src = lax.rem(z + 4 - d, 4)
        arrive(rows_full.at[src], b_send.at[d], b_recv.at[d])

    def columns(owner):
        return pl.ds(pl.multiple_of(lax.rem(owner, 2) * 512, 512), 512)

    for m in range(1, 8):
        to = flip(m)
        send(
            rows_full.at[lax.div(to, 2), :, columns(to)], rec_ref.at[lat],
            r_send.at[m], r_recv.at[m], lat=to,
        )
    rec_ref[lat] = rows_full[chip, :, columns(lat)]
    for i in range(4):
        gather_end(err_ref, i, e_send, e_recv)
    for m in range(1, 8):
        arrive(tc_ref.at[flip(m)], t_send.at[m], t_recv.at[m])
        arrive(rec_ref.at[flip(m)], r_send.at[m], r_recv.at[m])
    for copy in started:
        copy.wait_send()


def select_kernel(ids, place, *refs):
    out_ref = refs[-1]
    for n, ref in enumerate(refs[:-1]):
        at = (n * LAT_TILE) % out_ref.shape[1]
        out_ref[n * LAT_TILE // out_ref.shape[1], at : at + LAT_TILE] = ref[...]


def select(ids, place, dictionary, cap, group, width):
    blocks, depth = ids.size // cap, cap * LAT_TILE

    def row_spec(n):
        return pl.BlockSpec((LAT_TILE, width), lambda b, i, p: (i[b * group * cap + n], p[0]))

    return pl.pallas_call(
        select_kernel,
        out_shape=jax.ShapeDtypeStruct((blocks, depth, width), jnp.bfloat16),
        grid_spec=pltpu.PrefetchScalarGridSpec(
            num_scalar_prefetch=2,
            grid=(blocks // group,),
            in_specs=[row_spec(n) for n in range(group * cap)],
            out_specs=pl.BlockSpec((group, depth, width), lambda b, i, p: (b, 0, 0)),
        ),
        compiler_params=pltpu.CompilerParams(vmem_limit_bytes=VMEM_BYTES),
        cost_estimate=pl.CostEstimate(
            flops=0, bytes_accessed=4 * blocks * depth * width, transcendentals=0
        ),
        name="select",
    )(ids, place.reshape(1), *([dictionary] * (group * cap)))


def small_body(residuals, dictionary, enc_bias, dec_bias, tile_ids, tile_counts):
    cap = tile_ids.shape[2]
    lat_rows, model = dictionary.shape
    ids = tile_ids.reshape(-1)
    pieces = [ids] + [
        lax.ppermute(ids, "tok", [(n, (n + d) % 4) for n in range(4)]) for d in range(1, 4)
    ]
    group = jnp.arange(4, dtype=jnp.int32)[:, None]
    from_group = lax.rem(lax.axis_index("tok") + 4 - group, 4)
    ids_all = sum(jnp.where(from_group == d, pieces[d][None, :], 0) for d in range(4)).reshape(-1)
    rows_sel = select(ids, jnp.zeros((), jnp.int32), dictionary, cap, 1, model)
    cols_sel = select(ids_all, lax.axis_index("tok"), dictionary, cap, 2, 1024)
    bias = enc_bias.reshape(-1, LAT_TILE)[ids].reshape(4, 1, cap * LAT_TILE)
    live = jnp.arange(cap, dtype=jnp.int32)[None, :] < tile_counts
    live = jnp.repeat(live.astype(jnp.float32), LAT_TILE, axis=1).reshape(4, 1, cap * LAT_TILE)
    bf16, f32, dma = jnp.bfloat16, jnp.float32, pltpu.SemaphoreType.DMA
    vmem, anywhere = pl.BlockSpec(memory_space=pltpu.VMEM), pl.BlockSpec(memory_space=pl.ANY)
    codes_all, err_all, tiles, recon = pl.pallas_call(
        functools.partial(step_kernel, cap),
        out_shape=[
            jax.ShapeDtypeStruct((16, 128, cap * LAT_TILE), bf16),
            jax.ShapeDtypeStruct((8, 4, 64, 1024), bf16),
            jax.ShapeDtypeStruct((8, 4, 16, cap * LAT_TILE), bf16),
            jax.ShapeDtypeStruct((8, 64, 512), bf16),
        ],
        in_specs=[vmem, anywhere, anywhere, vmem, vmem, vmem],
        out_specs=[vmem, vmem, vmem, vmem],
        scratch_shapes=[
            pltpu.VMEM(rows_sel.shape, bf16),
            pltpu.VMEM(cols_sel.shape, bf16),
            pltpu.VMEM((8, 4, 128, 512), bf16),
            pltpu.VMEM((4, 4, 128, 1024), bf16),
            pltpu.VMEM((4, 4, 64, 1024), bf16),
        ]
        + [pltpu.VMEM((2, 64, 1024), bf16)] * 6
        + [
            pltpu.VMEM((4, 2, 64, 512), bf16),
            pltpu.VMEM((4, 64, 1024), bf16),
            pltpu.VMEM((4, 64, 1024), bf16),
            dma, dma,
            dma((4, 7)), dma((4, 8)), dma((4, 7)), dma((4, 8)),
            dma((4, 4)), dma((4, 4)),
            dma((4,)), dma((4,)),
            dma((8,)), dma((8,)),
            dma((4,)), dma((4,)),
            dma((6,)), dma((6,)),
            dma((4,)), dma((4,)),
            dma((8,)), dma((8,)),
        ],
        compiler_params=pltpu.CompilerParams(
            collective_id=0, has_side_effects=True, vmem_limit_bytes=VMEM_BYTES
        ),
        name="step",
    )(
        residuals.reshape(4, 128, 512),
        rows_sel,
        cols_sel,
        bias,
        dec_bias.reshape(8, 1, 512),
        live,
    )
    decoder_grad = grad(codes_all, ids_all, err_all, lat_rows)
    tiles = tiles.reshape(8, 4, 16, cap, LAT_TILE).transpose(1, 0, 3, 2, 4).reshape(4, 8, cap, -1)
    return tiles, recon.reshape(512, 512), decoder_grad


def solution(mesh):
    sizes = dict(mesh.shape)
    chosen = small_body if sizes == {"tok": 4, "lat": 8} else body
    placed = (
        P("tok", "lat"),
        P("lat", None),
        P("lat"),
        P(),
        P("tok", "lat", None),
        P("tok", "lat"),
    )
    return jax.shard_map(
        chosen,
        mesh=mesh,
        in_specs=placed,
        out_specs=(P("tok", None, None, "lat"), P("tok", "lat"), P("lat", "tok")),
        check_vma=False,
    )
```
